256 devices in a mesh: grp: 2 (over core), reg: 128 (over y, x, z).
Axes of the slice: x: 4, y: 4, z: 8, core: 2. Of those that a mesh axis runs over, the one named last changes fastest.
Arguments:
- anchors: float32 [3, 16384], P(None, ('grp', 'reg')), may hold values from -3 to 3
- directions: float32 [3, 16384], P(None, ('grp', 'reg')), may hold values from -4 to 4
- targets: float32 [3, 16384], P(None, ('grp', 'reg')), may hold values from 0 to 1
- region_ids: int32 [16384, 4], P(('grp', 'reg')), may hold values from 0 to 255, all different within a row; in each aligned block of 64 rows (0 to 63, 64 to 127, ...) at most 2 rows name the same one
- sample_counts: int32 [16384, 4], P(('grp', 'reg')), may hold values from 1 to 8
- depth_index: int32 [16384, 4, 8], P(('grp', 'reg')), may hold values from 0 to 127
- frequencies: float32 [3, 128], replicated, may hold values from -6 to 6
- w_input: bfloat16 [256, 256, 256], P(('grp', 'reg')), may hold values from -0.375 to 0.375
- w_hidden: bfloat16 [256, 2, 256, 256], P(('grp', 'reg')), may hold values from -0.375 to 0.375
- w_head: bfloat16 [256, 256, 4], P(('grp', 'reg')), may hold values from -0.375 to 0.375
Outputs:
- colours: float32 [3, 16384], P(None, ('grp', 'reg'))
- grad_input: bfloat16 [256, 256, 256], P(('grp', 'reg'))
- grad_hidden: bfloat16 [256, 2, 256, 256], P(('grp', 'reg'))
- grad_head: bfloat16 [256, 256, 4], P(('grp', 'reg'))
The draws below stay inside these ranges and needn't reach their ends.
Inputs may be any that keep to these rules, and one draw needn't show every extreme that they name: `region_ids`: within the rays of one device no region is named by more than 2 segments, a bound that some block reaches; the 4 segments of one ray name different regions.
All inputs are finite; a program needn't handle non-finite values.
Results may differ from the reference program's by a relative error of at most 0.015.
Values may be sent and summed in bfloat16 or wider, within the bound.
A program may use at most 64 MiB of HBM per device.

```python
import math
import jax
import jax.numpy as jnp
import numpy as np
from jax import lax

W = 256
LAYERS = 3
FREQ = 128
SEG = 4
SMP = 8
DEPTHS = 128
RAY_DEV = 64
REGIONS = 256
RAYS = 16384
CAP = 2
N_GRP = 2
N_REG = 128


def touch_ends(drawn, key, smallest, largest):
    longest = drawn.shape.index(max(drawn.shape))
    spots = []
    for shift in (0, 1):
        where = [jax.random.randint(jax.random.fold_in(key, axis), (), 0, length) for axis, length in enumerate(drawn.shape)]
        where[longest] = (where[longest] + shift) % drawn.shape[longest]
        spots.append(tuple(where))
    return drawn.at[spots[0]].set(smallest).at[spots[1]].set(largest)


def block_levels(stream_key, extent, shards, low, high):
    def one(dim, blocks):
        heights = jax.random.uniform(jax.random.fold_in(jax.random.fold_in(stream_key, 6), dim), (blocks,), jnp.float32, low / len(shards), high / len(shards))
        return jnp.repeat(jnp.exp(heights), extent[dim] // blocks).reshape((-1,) + (1,) * (len(extent) - dim - 1))

    factor_of = one(*shards[0])
    for cut in shards[1:]:
        factor_of = factor_of * one(*cut)
    return factor_of


def routed_block(key, own, number, rows, number_of, top, most, lean):
    order = jax.random.permutation(key, number_of)
    heavy_load, usual = shares(number_of, rows * top, most, lean, True), shares(number_of, rows * top, most, lean, False)
    places = jnp.arange(number_of)

    def named(sizes, turn):
        used = int((sizes > 0).sum())
        fixed = max(1, used // 4)
        shifted = fixed + (places - fixed + turn * (used - fixed)) % max(1, number_of - fixed)
        return jnp.zeros((number_of,), jnp.int32).at[order[jnp.where(places < fixed, places, shifted)]].set(jnp.asarray(sizes, jnp.int32))

    sizes = jnp.where(number % 4 == 0, named(heavy_load, number // 4), named(usual, number - number // 4 - 1))
    mixed = jax.random.permutation(jax.random.fold_in(own, 3), number_of)
    source_of, sink = mixed[0:number_of // 2 * 2:2], mixed[1:number_of // 2 * 2:2]
    slack = jnp.minimum(sizes[source_of] - 1, most - sizes[sink]) // 2
    slack = jnp.where((source_of == order[0]) | (sink == order[0]) | (sizes[sink] == 0), 0, jnp.maximum(slack, 0))
    shifted = jax.random.randint(jax.random.fold_in(own, 4), (number_of // 2,), 0, 1 << 20) % (slack + 1)
    sizes = sizes.at[source_of].add(-shifted).at[sink].add(shifted)
    labels = jnp.searchsorted(jnp.cumsum(sizes), jnp.arange(rows * top), side="right").astype(jnp.int32)
    table = labels.reshape(top, rows).T
    table = table[jax.random.permutation(jax.random.fold_in(own, 1), rows)]
    turn = jax.random.randint(jax.random.fold_in(own, 2), (rows, 1), 0, top)
    return jnp.take_along_axis(table, (jnp.arange(top)[None, :] + turn) % top, axis=1)


def shares(count, total, bound, lean, full):
    portions = [(1 << 20) // math.isqrt(grade ** lean) + 1 for grade in range(1, count + 1)]
    largest = bound if full else min(bound, max(-(-total // count), total * portions[0] // sum(portions)))
    least = 1 if total - largest >= count - 1 else 0
    holding, surplus = [largest] + [least] * (count - 1), total - largest - least * (count - 1)
    while surplus > 0:
        movable = [i for i in range(1, count) if holding[i] < largest] or [i for i in range(1, count) if holding[i] < bound]
        whole, remaining = sum([portions[i] for i in movable]), surplus
        for i in movable:
            addition = min(bound - holding[i], max(1, remaining * portions[i] // whole), surplus)
            holding[i] = holding[i] + addition
            surplus = surplus - addition
    return np.array(holding)


def centred(own_key, extent, spread, most, cuts=(), kind=jnp.bfloat16):
    values = spread * jax.random.normal(own_key, extent, jnp.float32)
    if cuts:
        values = values * block_levels(own_key, extent, cuts, -0.22, 0.18)
    return jnp.clip(values, -most, most).astype(kind)


def setup_inputs(seed: int = 0) -> dict:
    streams_of = jax.random.split(jax.random.key(seed), 11)
    anchors = centred(streams_of[0], (3, RAYS), 0.5, 3.0, ((1, 256),), jnp.float32)
    directions = centred(streams_of[1], (3, RAYS), 1.0, 4.0, ((1, 256),), jnp.float32)
    targets = jnp.clip(1.0 * jax.random.uniform(streams_of[2], (3, RAYS), jnp.float32) ** block_levels(streams_of[2], (3, RAYS), ((1, 256),), -0.2, 0.2), 0.0, 1.0)
    region_ids_keys = jax.random.split(jax.random.fold_in(streams_of[3], 1), RAYS // RAY_DEV)
    region_ids_turns = jax.random.permutation(jax.random.fold_in(streams_of[3], 3), RAYS // RAY_DEV)
    region_ids = jax.vmap(lambda own, number: routed_block(jax.random.fold_in(streams_of[3], 2), own, number, RAY_DEV, REGIONS, SEG, CAP, 2))(region_ids_keys, region_ids_turns).reshape((RAYS, SEG))
    sample_counts = touch_ends(jax.random.randint(streams_of[4], (RAYS, SEG), 1, SMP + 1), jax.random.fold_in(streams_of[4], 1), 1, SMP).astype(jnp.int32)
    depth_index = touch_ends(jax.random.randint(streams_of[5], (RAYS, SEG, SMP), 0, DEPTHS), jax.random.fold_in(streams_of[5], 1), 0, DEPTHS - 1).astype(jnp.int32)
    frequencies = centred(streams_of[6], (3, FREQ), 1.5, 6.0, (), jnp.float32)
    w_input = centred(streams_of[7], (REGIONS, 2 * FREQ, W), (2 * FREQ) ** -0.5, 0.375, ((0, 256),))
    w_hidden = centred(streams_of[8], (REGIONS, LAYERS - 1, W, W), W ** -0.5, 0.375, ((0, 256),))
    w_head = centred(streams_of[9], (REGIONS, W, 4), W ** -0.5, 0.375, ((0, 256),))
    return {"anchors": anchors, "directions": directions, "targets": targets, "region_ids": region_ids, "sample_counts": sample_counts, "depth_index": depth_index, "frequencies": frequencies, "w_input": w_input, "w_hidden": w_hidden, "w_head": w_head}


def depth_of(index):
    return 0.1 + (index.astype(jnp.float32) + 0.5) * (2.0 / DEPTHS)

def encode(anchor, direction, depth, frequencies):
    phases = None
    for column in range(3):
        position = anchor[..., column:column + 1] + depth * direction[..., column:column + 1]
        product_term = position[..., None] * frequencies[column]
        phases = product_term if phases is None else phases + product_term
    return jnp.concatenate([jnp.sin(phases), jnp.cos(phases)], axis=-1).astype(jnp.bfloat16)

def network(weights, encoded):
    first, middle, last = weights
    hidden = jax.nn.silu(jnp.dot(encoded, first, preferred_element_type=jnp.float32)).astype(jnp.bfloat16)
    for layer_index in range(middle.shape[0]):
        hidden = jax.nn.silu(jnp.dot(hidden, middle[layer_index], preferred_element_type=jnp.float32)).astype(jnp.bfloat16)
    return jnp.dot(hidden, last, preferred_element_type=jnp.float32)

def composite(values, live):
    sigma = jax.nn.softplus(values[..., 0])
    colour = jax.nn.sigmoid(values[..., 1:4])
    opacity = live * (1.0 - jnp.exp(-0.5 * sigma))
    through = jnp.cumprod(1.0 - opacity, axis=-1)
    before = jnp.concatenate([jnp.ones_like(through[..., :1]), through[..., :-1]], axis=-1)
    seg_colour = lax.optimization_barrier(jnp.sum((before * opacity)[..., None] * colour, axis=-2))
    return jnp.concatenate([seg_colour, through[..., -1:]], axis=-1)

def render(segments):
    through = jnp.cumprod(segments[..., 3], axis=-1)
    before = jnp.concatenate([jnp.ones_like(through[:, :1]), through[:, :-1]], axis=-1)
    return lax.optimization_barrier(jnp.sum(before[..., None] * segments[..., :3], axis=1)) + through[:, -1:]

def reference(anchors, directions, targets, region_ids, sample_counts, depth_index, frequencies, w_input, w_hidden, w_head):
    devices = N_GRP * N_REG
    per_device = RAY_DEV * SEG
    slots = devices * CAP
    region_block = region_ids.reshape(devices, per_device)
    owners = jnp.arange(REGIONS, dtype=jnp.int32)
    onehot = (region_block[:, :, None] == owners[None, None, :]).astype(jnp.int32)
    ranking = jnp.cumsum(onehot, axis=1) - onehot
    slot_index = lax.optimization_barrier(jnp.sum(ranking * onehot, axis=2)).astype(jnp.int32)
    position = (region_block * CAP + slot_index).astype(jnp.int32)
    sources = jnp.arange(devices, dtype=jnp.int32)
    global_index = (sources[:, None] * per_device + jnp.arange(per_device, dtype=jnp.int32)[None, :]).astype(jnp.int32)
    table = jnp.full((devices, REGIONS * CAP), -1, jnp.int32).at[sources[:, None], position].set(global_index)
    table = table.reshape(devices, REGIONS, CAP).transpose(1, 0, 2).reshape(REGIONS, slots)
    segment_anchor = jnp.repeat(anchors.T, SEG, axis=0)
    segment_direction = jnp.repeat(directions.T, SEG, axis=0)
    counts_flat = sample_counts.reshape(-1)
    depth_flat = depth_of(depth_index).reshape(-1, SMP)
    sample_iota = jnp.arange(SMP, dtype=jnp.int32)
    live_flat = (sample_iota[None, :] < counts_flat[:, None]).astype(jnp.float32)

    def slot_encoding(entries):
        safe = jnp.where(entries >= 0, entries, 0).astype(jnp.int32)
        encoded = encode(segment_anchor[safe], segment_direction[safe], depth_flat[safe], frequencies)
        return encoded.reshape(slots * SMP, 2 * FREQ)

    def forward_region(inputs):
        entries, first, middle, last = inputs
        return network((first, middle, last), slot_encoding(entries)).reshape(slots, SMP, 4)
    raw_all = lax.map(forward_region, (table, w_input, w_hidden, w_head))
    region_flat = region_ids.reshape(-1).astype(jnp.int32)
    source_flat = jnp.repeat(sources, per_device).astype(jnp.int32)
    flat_slot = (region_flat * slots + source_flat * CAP + slot_index.reshape(-1)).astype(jnp.int32)
    segment_raw = raw_all.reshape(REGIONS * slots, SMP, 4)[flat_slot]

    def render_all(values):
        return render(composite(values, live_flat).reshape(RAYS, SEG, 4))
    colours, render_pull = jax.vjp(render_all, segment_raw)
    raw_cotangent = render_pull(colours - targets.T)[0]
    cotangent_all = jnp.zeros((REGIONS * slots, SMP, 4), raw_cotangent.dtype).at[flat_slot].set(raw_cotangent)
    cotangent_all = cotangent_all.reshape(REGIONS, slots, SMP, 4)

    def backward_region(inputs):
        entries, first, middle, last, cotangent = inputs
        encoded = slot_encoding(entries)
        outputs, network_pull = jax.vjp(lambda weights: network(weights, encoded), (first, middle, last))
        return network_pull(cotangent.reshape(slots * SMP, 4))[0]
    grad_input, grad_hidden, grad_head = lax.map(backward_region, (table, w_input, w_hidden, w_head, cotangent_all))
    return (colours.T, grad_input, grad_hidden, grad_head)
```

```python
import functools
import math

import jax
import jax.numpy as jnp
from jax import lax
from jax.experimental import pallas as pl
from jax.experimental.pallas import tpu as pltpu
from jax.sharding import PartitionSpec as P

DEPTHS = 128
CHIPS_Z = 8
LANES = 128
MESH = pl.DeviceIdType.MESH
F32 = jnp.float32
BF16 = jnp.bfloat16

SIN = (6.283182621002197, -41.34142303466797, 81.59620666503906, -76.58030700683594,
       41.2061653137207, -12.272321701049805)
COS = (1.0, -19.73920440673828, 64.93911743164062, -85.45016479492188, 60.16783142089844,
       -25.968313217163086, 6.529609680175781)


def horner(coefficients, x):
    total = jnp.full_like(x, coefficients[-1])
    for value in coefficients[-2::-1]:
        total = total * x + value
    return total


def dot(a, b):
    return jnp.dot(a, b, preferred_element_type=F32)


def dot_nt(a, b):
    return lax.dot_general(a, b, (((1,), (1,)), ((), ())), preferred_element_type=F32)


def pieces(x):
    high = x.astype(BF16).astype(F32)
    rest = x - high
    middle = rest.astype(BF16).astype(F32)
    return high, middle, (rest - middle).astype(BF16).astype(F32)


def copies(source, target, rows, count, me, device, sends, receives):
    def outgoing(step):
        peer = lax.rem(me + step, count)
        return pltpu.make_async_remote_copy(
            src_ref=source.at[pl.ds(pl.multiple_of(peer * rows, rows), rows)],
            dst_ref=target.at[pl.ds(pl.multiple_of(me * rows, rows), rows)],
            send_sem=sends.at[peer],
            recv_sem=receives.at[me],
            device_id=device(peer),
            device_id_type=MESH,
        )

    def incoming(step):
        peer = lax.rem(me + step, count)
        part = target.at[pl.ds(pl.multiple_of(peer * rows, rows), rows)]
        return pltpu.make_async_remote_copy(
            src_ref=part,
            dst_ref=part,
            send_sem=sends.at[peer],
            recv_sem=receives.at[peer],
            device_id=device(peer),
            device_id_type=MESH,
        )

    return outgoing, incoming


def each(count, act):
    def body(step, carry):
        act(step)
        return carry

    lax.fori_loop(1, count, body, 0)


def exchange(source, target, rows, count, me, device, sends, receives):
    outgoing, incoming = copies(source, target, rows, count, me, device, sends, receives)
    each(count, lambda step: outgoing(step).start())
    own = pl.ds(pl.multiple_of(me * rows, rows), rows)
    target[own, :] = source[own, :]
    return (
        lambda: each(count, lambda step: incoming(step).wait_recv()),
        lambda: each(count, lambda step: outgoing(step).wait_send()),
    )


def turned(source, target, major, minor):
    for index in range(minor):
        target[index * major : (index + 1) * major, :] = source[
            pl.ds(index, major, stride=minor), :
        ]


def kernel(
    sizes,
    anchors, directions, targets, regions, counts, depths, frequencies, w_in, w_hid, w_head,
    colours, g_in, g_hid, g_head,
    send1, mid1, turn1, last1, send2, mid2, turn2, last2, send3, mid3, turn3, last3,
    rows_s, words_s, words_b, onehot, target_s, freq_s, slots_s, phase0, phase1, depth_s, head_s,
    raw_s, graw_s, cot_b, w1, wh, w1t, w2t, w3t, w2, w3, wot, wo, encoded, hidden, slope,
    acc1, acc2, acc3, acc4, sends, receives, local,
):
    groups, regs, zn, rays, segs, samples = sizes
    n = groups * regs
    near, far = groups * zn, regs // zn
    slots = 2 * n
    width = segs * LANES
    features = w_hid.shape[-1]
    freqs = features // 2

    grp = lax.axis_index("grp").astype(jnp.int32)
    reg = lax.axis_index("reg").astype(jnp.int32)
    me_far = lax.div(reg, zn)
    me_z = lax.rem(reg, zn)
    me_near = grp * zn + me_z

    def near_device(index):
        return (lax.div(index, zn), me_far * zn + lax.rem(index, zn))

    def far_device(index):
        return (grp, index * zn + me_z)

    barrier = pltpu.get_barrier_semaphore()

    def greet(count, me, device):
        def act(step):
            pl.semaphore_signal(
                barrier, inc=1, device_id=device(lax.rem(me + step, count)), device_id_type=MESH
            )

        each(count, act)

    greet(near, me_near, near_device)
    greet(far, me_far, far_device)

    load_in = pltpu.make_async_copy(w_in.at[0], w1, local.at[0])
    load_hid = pltpu.make_async_copy(w_hid.at[0], wh, local.at[1])
    load_in.start()
    load_hid.start()

    ids = regions[...]
    in_group = lax.rem(ids, regs)
    place = (lax.div(ids, regs) * zn + lax.rem(in_group, zn)) * far + lax.div(in_group, zn)
    rows_s[...] = jnp.full(rows_s.shape, -1, jnp.int32)
    words_s[...] = jnp.zeros(words_s.shape, F32)
    for k in range(segs):
        part = slice(k * LANES, k * LANES + rays)
        rows_s[0:1, part] = place[k : k + 1]
        both = jnp.concatenate([anchors[...], directions[...]], axis=0)
        high, middle, low = pieces(both)
        words_s[0:6, part] = high
        words_s[6:12, part] = middle
        words_s[12:18, part] = low
        words_s[18:19, part] = counts[k : k + 1].astype(F32)
        words_s[24 : 24 + samples, part] = depths[k].astype(F32)
    row_of = rows_s[0:1, :]
    match = row_of == lax.broadcasted_iota(jnp.int32, (n, width), 0)
    number = lax.broadcasted_iota(jnp.int32, (n, width), 1)
    last = jnp.max(jnp.where(match, number, -1), axis=1, keepdims=True)
    first_slot = number == last
    onehot[:, 0:width] = jnp.where(first_slot, 1.0, 0.0).astype(BF16)
    onehot[:, width:] = jnp.where(match & jnp.logical_not(first_slot), 1.0, 0.0).astype(BF16)
    words_b[...] = jnp.zeros(words_b.shape, BF16)
    packed = words_s[...].astype(BF16)
    words_b[0:32, 0:width] = packed
    words_b[32:64, width:] = packed
    send1[...] = dot_nt(onehot[...], words_b[...])

    pl.semaphore_wait(barrier, near + far - 2)

    wait_near1, sent_near1 = exchange(
        send1, mid1, far, near, me_near, near_device, sends.at[0], receives.at[0]
    )
    load_in.wait()
    load_hid.wait()
    w1t[...] = (w1[...].astype(F32) * 0.5).T.astype(BF16)
    half2 = wh[0].astype(F32) * 0.5
    w2[...] = half2.astype(BF16)
    w2t[...] = half2.T.astype(BF16)
    half3 = wh[1].astype(F32) * 0.5
    w3[...] = half3.astype(BF16)
    w3t[...] = half3.T.astype(BF16)
    wait_near1()
    turned(mid1, turn1, near, far)
    wait_far1, sent_far1 = exchange(
        turn1, last1, near, far, me_far, far_device, sends.at[1], receives.at[1]
    )
    head_s[...] = jnp.zeros(head_s.shape, F32)
    head_s[0:4, :] = w_head[...].astype(F32)
    wot[...] = head_s[...].astype(BF16)
    wo[...] = (head_s[...] * 0.5).T.astype(BF16)
    freq_s[...] = jnp.zeros(freq_s.shape, F32)
    freq_s[0:3, :] = frequencies[...] * (1.0 / (2.0 * math.pi))
    columns = freq_s[...].T
    send2[...] = jnp.zeros(send2.shape, F32)
    send3[...] = jnp.zeros(send3.shape, F32)
    graw_s[...] = jnp.zeros(graw_s.shape, F32)
    cot_b[...] = jnp.zeros(cot_b.shape, BF16)
    target_s[...] = jnp.zeros(target_s.shape, F32)
    target_s[0:3, 0:rays] = targets[...]
    acc1[...] = jnp.zeros(acc1.shape, F32)
    acc2[...] = jnp.zeros(acc2.shape, F32)
    acc3[...] = jnp.zeros(acc3.shape, F32)
    acc4[...] = jnp.zeros(acc4.shape, F32)
    wait_far1()

    words = last1[...].T
    slots_s[:, 0:n] = words[0:32]
    slots_s[:, n:] = words[32:64]
    geometry = (slots_s[0:6, :] + slots_s[6:12, :]) + slots_s[12:18, :]
    base = jnp.zeros((freqs, slots), F32)
    rate = jnp.zeros((freqs, slots), F32)
    for c in range(3):
        base = base + columns[:, c : c + 1] * geometry[c : c + 1]
        rate = rate + columns[:, c : c + 1] * geometry[3 + c : 4 + c]
    phase0[...] = base
    phase1[...] = rate
    depth_s[...] = 0.1 + (slots_s[24 : 24 + samples, :] + 0.5) * (2.0 / DEPTHS)
    live = jnp.where(
        lax.broadcasted_iota(jnp.int32, (samples, slots), 0).astype(F32) < slots_s[18:19, :],
        1.0, 0.0,
    )

    def layer(index, j, weights, x):
        z = dot(weights, x)
        t = jnp.tanh(z)
        h = z + z * t
        hidden[index, j] = h.astype(BF16)
        slope[index, j] = ((1.0 + h) + t * (1.0 - h)).astype(BF16)
        return h.astype(BF16)

    def forward(j, carry):
        turns = phase0[...] + depth_s[pl.ds(j, 1), :] * phase1[...]
        r = turns - jnp.round(turns)
        square = r * r
        x = jnp.concatenate([r * horner(SIN, square), horner(COS, square)], axis=0).astype(BF16)
        encoded[j] = x
        x = layer(0, j, w1t[...], x)
        x = layer(1, j, w2t[...], x)
        x = layer(2, j, w3t[...], x)
        raw = dot(wot[...], x)
        for k in range(4):
            raw_s[k, pl.ds(j, 1), :] = raw[k : k + 1]
        return carry

    lax.fori_loop(0, samples, forward, 0)

    density = raw_s[0]
    small = jnp.exp(-jnp.abs(density))
    softplus = jnp.maximum(density, 0.0) + jnp.log1p(small)
    clear = jnp.exp(-0.5 * softplus)
    alpha = live * (1.0 - clear)
    keep = 1.0 - alpha
    tone = [jax.nn.sigmoid(raw_s[1 + c]) for c in range(3)]
    through = jnp.ones((1, slots), F32)
    befores = []
    for i in range(samples):
        befores.append(through)
        through = through * keep[i : i + 1]
    before = jnp.concatenate(befores, axis=0)
    weight = before * alpha
    seg = [jnp.sum(weight * tone[c], axis=0, keepdims=True) for c in range(3)] + [through]
    answer = jnp.concatenate(
        [part[:, 0:n] for part in seg] + [part[:, n:] for part in seg], axis=0
    )
    send2[:, 0:8] = answer.T

    wait_far2, sent_far2 = exchange(
        send2, mid2, near, far, me_far, far_device, sends.at[2], receives.at[2]
    )
    d_density = 0.5 * live * clear * jnp.where(density >= 0.0, 1.0, small) / (1.0 + small)
    d_tone = [weight * t * (1.0 - t) for t in tone]
    wait_far2()
    turned(mid2, turn2, far, near)
    wait_near2, sent_near2 = exchange(
        turn2, last2, far, near, me_near, near_device, sends.at[3], receives.at[3]
    )
    wait_near2()

    values = last2[...].T[0:8]
    high, middle, low = pieces(values)
    blank = jnp.zeros((4, n), F32)
    left = jnp.concatenate([high[0:4], middle[0:4], low[0:4], blank], axis=0).astype(BF16)
    right = jnp.concatenate([high[4:8], middle[4:8], low[4:8], blank], axis=0).astype(BF16)
    found = dot(left, onehot[:, 0:width]) + dot(right, onehot[:, width:])
    found = (found[0:4] + found[4:8]) + found[8:12]
    arrive = [jnp.ones((1, LANES), F32)]
    total = jnp.zeros((3, LANES), F32)
    parts = []
    for k in range(segs):
        part = found[:, k * LANES : (k + 1) * LANES]
        parts.append(part)
        total = total + arrive[k] * part[0:3]
        arrive.append(arrive[k] * part[3:4])
    total = total + arrive[segs]
    colours[...] = total[:, 0:rays]
    error = total - target_s[0:3, :]
    behind = jnp.sum(error, axis=0, keepdims=True)
    for k in range(segs - 1, -1, -1):
        part = parts[k]
        cotangent = jnp.concatenate([arrive[k] * error, arrive[k] * behind], axis=0)
        behind = jnp.sum(error * part[0:3], axis=0, keepdims=True) + part[3:4] * behind
        stack = jnp.concatenate(
            list(pieces(cotangent)) + [jnp.zeros((4, LANES), F32)], axis=0
        ).astype(BF16)
        cot_b[0:16, k * LANES : (k + 1) * LANES] = stack
        cot_b[16:32, width + k * LANES : width + (k + 1) * LANES] = stack
    send3[:, 0:32] = dot_nt(onehot[...], cot_b[...])

    wait_near3, sent_near3 = exchange(
        send3, mid3, far, near, me_near, near_device, sends.at[4], receives.at[4]
    )
    wait_near3()
    turned(mid3, turn3, near, far)
    wait_far3, sent_far3 = exchange(
        turn3, last3, near, far, me_far, far_device, sends.at[5], receives.at[5]
    )
    wait_far3()

    words = last3[...].T[0:32]
    given = jnp.concatenate(
        [(words[0:4] + words[4:8]) + words[8:12], (words[16:20] + words[20:24]) + words[24:28]],
        axis=1,
    )
    gain = given[0:1] * tone[0] + given[1:2] * tone[1] + given[2:3] * tone[2]
    after = given[3:4]
    backs = []
    for i in range(samples - 1, -1, -1):
        backs.append(befores[i] * (gain[i : i + 1] - after))
        after = alpha[i : i + 1] * gain[i : i + 1] + keep[i : i + 1] * after
    d_raw = [jnp.concatenate(backs[::-1], axis=0) * d_density]
    d_raw += [given[c : c + 1] * d_tone[c] for c in range(3)]
    for j in range(samples):
        for k in range(4):
            graw_s[j, k : k + 1, :] = d_raw[k][j : j + 1]

    def backward(j, carry):
        g = graw_s[j].astype(BF16)
        h3 = hidden[2, j]
        acc4[...] += dot_nt(g, h3)
        g = (dot(wo[...], g) * slope[2, j].astype(F32)).astype(BF16)
        acc3[...] += dot_nt(hidden[1, j], g)
        g = (dot(w3[...], g) * slope[1, j].astype(F32)).astype(BF16)
        acc2[...] += dot_nt(hidden[0, j], g)
        g = (dot(w2[...], g) * slope[0, j].astype(F32)).astype(BF16)
        acc1[...] += dot_nt(encoded[j], g)
        return carry

    lax.fori_loop(0, samples, backward, 0)
    g_in[0] = acc1[...].astype(BF16)
    g_hid[0, 0] = acc2[...].astype(BF16)
    g_hid[0, 1] = acc3[...].astype(BF16)
    g_head[...] = acc4[0:4, :].astype(BF16)

    for sent in (sent_near1, sent_far1, sent_far2, sent_near2, sent_near3, sent_far3):
        sent()


def per_device(
    anchors, directions, targets, region_ids, sample_counts, depth_index, frequencies,
    w_input, w_hidden, w_head,
):
    groups, regs = lax.axis_size("grp"), lax.axis_size("reg")
    rays, segs = region_ids.shape
    samples = depth_index.shape[2]
    width = w_input.shape[1]
    zn = min(CHIPS_Z, regs)
    n = groups * regs
    slots = 2 * n
    near, far = groups * zn, regs // zn
    peers = max(near, far)
    lanes = segs * LANES
    board = [pltpu.VMEM((n, LANES), F32)] * 12
    square = (width, width)
    scratch = board + [
        pltpu.VMEM((8, lanes), jnp.int32),
        pltpu.VMEM((32, lanes), F32),
        pltpu.VMEM((LANES, 2 * lanes), BF16),
        pltpu.VMEM((n, 2 * lanes), BF16),
        pltpu.VMEM((8, LANES), F32),
        pltpu.VMEM((8, width // 2), F32),
        pltpu.VMEM((32, slots), F32),
        pltpu.VMEM((width // 2, slots), F32),
        pltpu.VMEM((width // 2, slots), F32),
        pltpu.VMEM((samples, slots), F32),
        pltpu.VMEM((16, width), F32),
        pltpu.VMEM((4, samples, slots), F32),
        pltpu.VMEM((samples, 16, slots), F32),
        pltpu.VMEM((32, 2 * lanes), BF16),
        pltpu.VMEM(square, BF16),
        pltpu.VMEM((2,) + square, BF16),
        pltpu.VMEM(square, BF16),
        pltpu.VMEM(square, BF16),
        pltpu.VMEM(square, BF16),
        pltpu.VMEM(square, BF16),
        pltpu.VMEM(square, BF16),
        pltpu.VMEM((16, width), BF16),
        pltpu.VMEM((width, 16), BF16),
        pltpu.VMEM((samples, width, slots), BF16),
        pltpu.VMEM((3, samples, width, slots), BF16),
        pltpu.VMEM((3, samples, width, slots), BF16),
        pltpu.VMEM(square, F32),
        pltpu.VMEM(square, F32),
        pltpu.VMEM(square, F32),
        pltpu.VMEM((16, width), F32),
        pltpu.SemaphoreType.DMA((6, peers)),
        pltpu.SemaphoreType.DMA((6, peers)),
        pltpu.SemaphoreType.DMA((2,)),
    ]
    vmem = pl.BlockSpec(memory_space=pltpu.VMEM)
    whole = pl.BlockSpec(memory_space=pl.ANY)
    colours, g_in, g_hid, g_head = pl.pallas_call(
        functools.partial(kernel, (groups, regs, zn, rays, segs, samples)),
        out_shape=(
            jax.ShapeDtypeStruct((3, rays), F32),
            jax.ShapeDtypeStruct(w_input.shape, BF16),
            jax.ShapeDtypeStruct(w_hidden.shape, BF16),
            jax.ShapeDtypeStruct((4, width), BF16),
        ),
        in_specs=[vmem] * 7 + [whole, whole, vmem],
        out_specs=[vmem] * 4,
        scratch_shapes=scratch,
        compiler_params=pltpu.CompilerParams(
            collective_id=0, has_side_effects=True, vmem_limit_bytes=48 * 1024 * 1024
        ),
        name="radiance_step",
    )(
        anchors, directions, targets, region_ids.T, sample_counts.T,
        depth_index.transpose(1, 2, 0), frequencies, w_input, w_hidden, w_head[0].T,
    )
    return colours, g_in, g_hid, g_head.T[None]


def solution(mesh):
    both = ("grp", "reg")
    return jax.shard_map(
        per_device,
        mesh=mesh,
        in_specs=(
            P(None, both), P(None, both), P(None, both), P(both, None), P(both, None),
            P(both, None, None), P(), P(both, None, None), P(both, None, None, None),
            P(both, None, None),
        ),
        out_specs=(
            P(None, both), P(both, None, None), P(both, None, None, None), P(both, None, None),
        ),
        check_vma=False,
    )
```

```python
import functools
import math

import jax
import jax.numpy as jnp
from jax import lax
from jax.experimental import pallas as pl
from jax.experimental.pallas import tpu as pltpu
from jax.sharding import PartitionSpec as P

DEPTHS = 128
CHIPS_Z = 8
VMEM_BYTES = 64 * 1024 * 1024
LANES = 128
MESH = pl.DeviceIdType.MESH
F32 = jnp.float32
BF16 = jnp.bfloat16

SIN = (6.283182621002197, -41.34142303466797, 81.59620666503906, -76.58030700683594,
       41.2061653137207, -12.272321701049805)
COS = (1.0, -19.73920440673828, 64.93911743164062, -85.45016479492188, 60.16783142089844,
       -25.968313217163086, 6.529609680175781)


def horner(coefficients, x):
    total = jnp.full_like(x, coefficients[-1])
    for value in coefficients[-2::-1]:
        total = total * x + value
    return total


def dot(a, b):
    return jnp.dot(a, b, preferred_element_type=F32)


def dot_nt(a, b):
    return lax.dot_general(a, b, (((1,), (1,)), ((), ())), preferred_element_type=F32)


def pieces(x):
    high = x.astype(BF16).astype(F32)
    rest = x - high
    middle = rest.astype(BF16).astype(F32)
    return high, middle, (rest - middle).astype(BF16).astype(F32)


def exchange(source, target, rows, count, me, device, send, receive):
    def part(ref, index):
        return ref.at[pl.ds(pl.multiple_of(index * rows, rows), rows)]

    for step in range(1, count):
        peer = lax.rem(me + step, count)
        pltpu.make_async_remote_copy(
            src_ref=part(source, peer),
            dst_ref=part(target, me),
            send_sem=send,
            recv_sem=receive,
            device_id=device(peer),
            device_id_type=MESH,
        ).start()
    own = pl.ds(pl.multiple_of(me * rows, rows), rows)
    target[own, :] = source[own, :]
    others = pl.ds(0, (count - 1) * rows)
    everything = pltpu.make_async_remote_copy(
        src_ref=source.at[others],
        dst_ref=target.at[others],
        send_sem=send,
        recv_sem=receive,
        device_id=device(lax.rem(me + 1, count)),
        device_id_type=MESH,
    )
    return everything.wait_recv, everything.wait_send


def turned(source, loose, target, major, minor):
    loose[...] = source[...].astype(F32)
    for index in range(minor):
        target[index * major : (index + 1) * major, :] = loose[
            pl.ds(index, major, stride=minor), :
        ].astype(BF16)


def staged(stages, count):
    for step in range(count + stages - 1):
        for stage in range(stages):
            if 0 <= step - stage < count:
                yield stage, step - stage


def kernel(
    sizes,
    *refs,
):
    arguments, results = refs[:10], refs[10:14]
    (
    send1, mid1, turn1, last1, send2, mid2, turn2, last2, send3, mid3, turn3, last3,
    loose, rows_s, words_s, words_b, onehot, target_s, freq_s, slots_s, phase0, phase1, depth_s, head_s,
    raw_s, graw_s, cot_b, w1t, w2t, w3t, w2, w3, wot, wo, encoded, hidden, slope, cotangents,
    acc1, acc2, acc3, acc4, colours, g_in, g_hid, g_head, sends, receives, local,
    ) = refs[24:]
    held = refs[14:24]
    anchors, directions, targets, regions, counts, depths, frequencies, w1, wh, w_head = held
    made = (colours, g_in, g_hid, g_head)
    groups, regs, zn, rays, segs, samples = sizes
    loads = [
        pltpu.make_async_copy(argument, place, local.at[index])
        for index, (argument, place) in enumerate(zip(arguments, held))
    ]
    for load in loads:
        load.start()
    n = groups * regs
    near, far = groups * zn, regs // zn
    slots = 2 * n
    width = segs * LANES
    features = wh.shape[-1]
    freqs = features // 2

    grp = lax.axis_index("grp").astype(jnp.int32)
    reg = lax.axis_index("reg").astype(jnp.int32)
    me_far = lax.div(reg, zn)
    me_z = lax.rem(reg, zn)
    me_near = grp * zn + me_z

    def near_device(index):
        return (lax.div(index, zn), me_far * zn + lax.rem(index, zn))

    def far_device(index):
        return (grp, index * zn + me_z)

    barrier = pltpu.get_barrier_semaphore()

    for count, me, device in ((near, me_near, near_device), (far, me_far, far_device)):
        for step in range(1, count):
            pl.semaphore_signal(
                barrier, inc=1, device_id=device(lax.rem(me + step, count)), device_id_type=MESH
            )
    for index in (0, 1, 3, 4, 5):
        loads[index].wait()

    ids = regions[...]
    in_group = lax.rem(ids, regs)
    place = (lax.div(ids, regs) * zn + lax.rem(in_group, zn)) * far + lax.div(in_group, zn)
    rows_s[...] = jnp.full(rows_s.shape, -1, jnp.int32)
    words_s[...] = jnp.zeros(words_s.shape, F32)
    for k in range(segs):
        part = slice(k * LANES, k * LANES + rays)
        rows_s[0:1, part] = place[k : k + 1]
        both = jnp.concatenate([anchors[...], directions[...]], axis=0)
        high, middle, low = pieces(both)
        words_s[0:6, part] = high
        words_s[6:12, part] = middle
        words_s[12:18, part] = low
        words_s[18:19, part] = counts[k : k + 1].astype(F32)
        words_s[24 : 24 + samples, part] = depths[k].astype(F32)
    row_of = rows_s[0:1, :]
    match = row_of == lax.broadcasted_iota(jnp.int32, (n, width), 0)
    number = lax.broadcasted_iota(jnp.int32, (n, width), 1)
    last = jnp.max(jnp.where(match, number, -1), axis=1, keepdims=True)
    first_slot = number == last
    onehot[:, 0:width] = jnp.where(first_slot, 1.0, 0.0).astype(BF16)
    onehot[:, width:] = jnp.where(match & jnp.logical_not(first_slot), 1.0, 0.0).astype(BF16)
    words_b[...] = jnp.zeros(words_b.shape, BF16)
    packed = words_s[...].astype(BF16)
    words_b[0:32, 0:width] = packed
    words_b[32:64, width:] = packed
    send1[...] = dot_nt(onehot[...], words_b[...]).astype(BF16)

    pl.semaphore_wait(barrier, near + far - 2)

    wait_near1, sent_near1 = exchange(
        send1, mid1, far, near, me_near, near_device, sends.at[0], receives.at[0]
    )
    for index in (2, 6, 7, 8, 9):
        loads[index].wait()
    w1t[...] = (w1[0].astype(F32) * 0.5).T.astype(BF16)
    half2 = wh[0, 0].astype(F32) * 0.5
    w2[...] = half2.astype(BF16)
    w2t[...] = half2.T.astype(BF16)
    half3 = wh[0, 1].astype(F32) * 0.5
    w3[...] = half3.astype(BF16)
    w3t[...] = half3.T.astype(BF16)
    wait_near1()
    turned(mid1, loose, turn1, near, far)
    wait_far1, sent_far1 = exchange(
        turn1, last1, near, far, me_far, far_device, sends.at[1], receives.at[1]
    )
    head_s[...] = jnp.zeros(head_s.shape, F32)
    head_s[0:4, :] = w_head[...].astype(F32)
    wot[...] = head_s[...].astype(BF16)
    wo[...] = (head_s[...] * 0.5).T.astype(BF16)
    freq_s[...] = jnp.zeros(freq_s.shape, F32)
    freq_s[0:3, :] = frequencies[...] * (1.0 / (2.0 * math.pi))
    columns = freq_s[...].T
    send2[...] = jnp.zeros(send2.shape, BF16)
    send3[...] = jnp.zeros(send3.shape, BF16)
    graw_s[...] = jnp.zeros(graw_s.shape, F32)
    cot_b[...] = jnp.zeros(cot_b.shape, BF16)
    target_s[...] = jnp.zeros(target_s.shape, F32)
    target_s[0:3, 0:rays] = targets[...]
    wait_far1()

    words = last1[...].astype(F32).T
    slots_s[:, 0:n] = words[0:32]
    slots_s[:, n:] = words[32:64]
    geometry = (slots_s[0:6, :] + slots_s[6:12, :]) + slots_s[12:18, :]
    base = jnp.zeros((freqs, slots), F32)
    rate = jnp.zeros((freqs, slots), F32)
    for c in range(3):
        base = base + columns[:, c : c + 1] * geometry[c : c + 1]
        rate = rate + columns[:, c : c + 1] * geometry[3 + c : 4 + c]
    phase0[...] = base
    phase1[...] = rate
    depth_s[...] = 0.1 + (slots_s[24 : 24 + samples, :] + 0.5) * (2.0 / DEPTHS)
    live = jnp.where(
        lax.broadcasted_iota(jnp.int32, (samples, slots), 0).astype(F32) < slots_s[18:19, :],
        1.0, 0.0,
    )

    layers = (w1t, w2t, w3t)
    for stage, j in staged(5, samples):
        if stage == 0:
            turns = phase0[...] + depth_s[j : j + 1, :] * phase1[...]
            r = turns - jnp.round(turns)
            square = r * r
            encoded[j, 0:freqs] = (r * horner(SIN, square)).astype(BF16)
            encoded[j, freqs:] = horner(COS, square).astype(BF16)
        elif stage < 4:
            z = dot(layers[stage - 1][...], encoded[j] if stage == 1 else hidden[stage - 2, j])
            t = jnp.tanh(z)
            h = z + z * t
            hidden[stage - 1, j] = h.astype(BF16)
            slope[stage - 1, j] = ((1.0 + h) + t * (1.0 - h)).astype(BF16)
        else:
            raw = dot(wot[...], hidden[2, j])
            for k in range(4):
                raw_s[k, j : j + 1, :] = raw[k : k + 1]

    density = raw_s[0]
    small = jnp.exp(-jnp.abs(density))
    softplus = jnp.maximum(density, 0.0) + jnp.log1p(small)
    clear = jnp.exp(-0.5 * softplus)
    alpha = live * (1.0 - clear)
    keep = 1.0 - alpha
    tone = [jax.nn.sigmoid(raw_s[1 + c]) for c in range(3)]
    through = jnp.ones((1, slots), F32)
    befores = []
    for i in range(samples):
        befores.append(through)
        through = through * keep[i : i + 1]
    before = jnp.concatenate(befores, axis=0)
    weight = before * alpha
    seg = [jnp.sum(weight * tone[c], axis=0, keepdims=True) for c in range(3)] + [through]
    answer = jnp.concatenate(seg, axis=0)
    blank = jnp.zeros((4, slots), F32)
    answer = jnp.concatenate(list(pieces(answer)) + [blank], axis=0)
    answer = jnp.concatenate([answer[:, 0:n], answer[:, n:]], axis=0)
    send2[:, 0:32] = answer.T.astype(BF16)

    wait_far2, sent_far2 = exchange(
        send2, mid2, near, far, me_far, far_device, sends.at[2], receives.at[2]
    )
    d_density = 0.5 * live * clear * jnp.where(density >= 0.0, 1.0, small) / (1.0 + small)
    d_tone = [weight * t * (1.0 - t) for t in tone]
    wait_far2()
    turned(mid2, loose, turn2, far, near)
    wait_near2, sent_near2 = exchange(
        turn2, last2, far, near, me_near, near_device, sends.at[3], receives.at[3]
    )
    wait_near2()

    values = last2[...].astype(F32).T[0:32].astype(BF16)
    found = dot(values[0:16], onehot[:, 0:width]) + dot(values[16:32], onehot[:, width:])
    found = (found[0:4] + found[4:8]) + found[8:12]
    arrive = [jnp.ones((1, LANES), F32)]
    total = jnp.zeros((3, LANES), F32)
    parts = []
    for k in range(segs):
        part = found[:, k * LANES : (k + 1) * LANES]
        parts.append(part)
        total = total + arrive[k] * part[0:3]
        arrive.append(arrive[k] * part[3:4])
    total = total + arrive[segs]
    colours[...] = total[:, 0:rays]
    error = total - target_s[0:3, :]
    behind = jnp.sum(error, axis=0, keepdims=True)
    for k in range(segs - 1, -1, -1):
        part = parts[k]
        cotangent = jnp.concatenate([arrive[k] * error, arrive[k] * behind], axis=0)
        behind = jnp.sum(error * part[0:3], axis=0, keepdims=True) + part[3:4] * behind
        stack = jnp.concatenate(
            list(pieces(cotangent)) + [jnp.zeros((4, LANES), F32)], axis=0
        ).astype(BF16)
        cot_b[0:16, k * LANES : (k + 1) * LANES] = stack
        cot_b[16:32, width + k * LANES : width + (k + 1) * LANES] = stack
    send3[:, 0:32] = dot_nt(onehot[...], cot_b[...]).astype(BF16)

    wait_near3, sent_near3 = exchange(
        send3, mid3, far, near, me_near, near_device, sends.at[4], receives.at[4]
    )
    wait_near3()
    turned(mid3, loose, turn3, near, far)
    wait_far3, sent_far3 = exchange(
        turn3, last3, near, far, me_far, far_device, sends.at[5], receives.at[5]
    )
    wait_far3()

    words = last3[...].astype(F32).T[0:32]
    given = jnp.concatenate(
        [(words[0:4] + words[4:8]) + words[8:12], (words[16:20] + words[20:24]) + words[24:28]],
        axis=1,
    )
    gain = given[0:1] * tone[0] + given[1:2] * tone[1] + given[2:3] * tone[2]
    after = given[3:4]
    backs = []
    for i in range(samples - 1, -1, -1):
        backs.append(befores[i] * (gain[i : i + 1] - after))
        after = alpha[i : i + 1] * gain[i : i + 1] + keep[i : i + 1] * after
    d_raw = [jnp.concatenate(backs[::-1], axis=0) * d_density]
    d_raw += [given[c : c + 1] * d_tone[c] for c in range(3)]
    for j in range(samples):
        for k in range(4):
            graw_s[j, k : k + 1, :] = d_raw[k][j : j + 1]

    backs = (wo, w3, w2)
    inputs = (lambda j: hidden[1, j], lambda j: hidden[0, j], lambda j: encoded[j])
    totals = (acc3, acc2, acc1)

    def gather(total, j, term):
        if j == 0:
            total[...] = term
        else:
            total[...] += term

    for stage, j in staged(4, samples):
        if stage == 0:
            gather(acc4, j, dot_nt(graw_s[j].astype(BF16), hidden[2, j]))
        if stage < 3:
            g = graw_s[j].astype(BF16) if stage == 0 else cotangents[stage - 1, j]
            g = dot(backs[stage][...], g) * slope[2 - stage, j].astype(F32)
            cotangents[stage, j] = g.astype(BF16)
        if stage > 0:
            gather(totals[stage - 1], j, dot_nt(inputs[stage - 1](j), cotangents[stage - 1, j]))

    g_in[0] = acc1[...].astype(BF16)
    g_hid[0, 0] = acc2[...].astype(BF16)
    g_hid[0, 1] = acc3[...].astype(BF16)
    g_head[...] = acc4[0:4, :].astype(BF16)
    stores = [
        pltpu.make_async_copy(place, result, local.at[10 + index])
        for index, (place, result) in enumerate(zip(made, results))
    ]
    for store in stores:
        store.start()
    for store in stores:
        store.wait()

    for sent in (sent_near1, sent_far1, sent_far2, sent_near2, sent_near3, sent_far3):
        sent()


def hand_over(*refs):
    moves = [
        pltpu.make_async_copy(refs[index], refs[4 + index], refs[8].at[index])
        for index in range(4)
    ]
    for move in moves:
        move.start()
    for move in moves:
        move.wait()


def per_device(
    anchors, directions, targets, region_ids, sample_counts, depth_index, frequencies,
    w_input, w_hidden, w_head,
):
    groups, regs = lax.axis_size("grp"), lax.axis_size("reg")
    rays, segs = region_ids.shape
    samples = depth_index.shape[2]
    width = w_input.shape[1]
    zn = min(CHIPS_Z, regs)
    n = groups * regs
    slots = 2 * n
    near, far = groups * zn, regs // zn
    lanes = segs * LANES
    board = [pltpu.VMEM((n, LANES), BF16)] * 12
    square = (width, width)
    operands = (
        anchors, directions, targets, region_ids.T, sample_counts.T,
        depth_index.transpose(1, 2, 0), frequencies, w_input, w_hidden, w_head[0].T,
    )
    shapes = (
        jax.ShapeDtypeStruct((3, rays), F32),
        jax.ShapeDtypeStruct(w_input.shape, BF16),
        jax.ShapeDtypeStruct(w_hidden.shape, BF16),
        jax.ShapeDtypeStruct((4, width), BF16),
    )
    scratch = [pltpu.VMEM(x.shape, x.dtype) for x in operands] + board + [
        pltpu.VMEM((n, LANES), F32),
        pltpu.VMEM((8, lanes), jnp.int32),
        pltpu.VMEM((32, lanes), F32),
        pltpu.VMEM((LANES, 2 * lanes), BF16),
        pltpu.VMEM((n, 2 * lanes), BF16),
        pltpu.VMEM((8, LANES), F32),
        pltpu.VMEM((8, width // 2), F32),
        pltpu.VMEM((32, slots), F32),
        pltpu.VMEM((width // 2, slots), F32),
        pltpu.VMEM((width // 2, slots), F32),
        pltpu.VMEM((samples, slots), F32),
        pltpu.VMEM((16, width), F32),
        pltpu.VMEM((4, samples, slots), F32),
        pltpu.VMEM((samples, 16, slots), F32),
        pltpu.VMEM((32, 2 * lanes), BF16),
        pltpu.VMEM(square, BF16),
        pltpu.VMEM(square, BF16),
        pltpu.VMEM(square, BF16),
        pltpu.VMEM(square, BF16),
        pltpu.VMEM(square, BF16),
        pltpu.VMEM((16, width), BF16),
        pltpu.VMEM((width, 16), BF16),
        pltpu.VMEM((samples, width, slots), BF16),
        pltpu.VMEM((3, samples, width, slots), BF16),
        pltpu.VMEM((3, samples, width, slots), BF16),
        pltpu.VMEM((3, samples, width, slots), BF16),
        pltpu.VMEM(square, F32),
        pltpu.VMEM(square, F32),
        pltpu.VMEM(square, F32),
        pltpu.VMEM((16, width), F32),
    ] + [pltpu.VMEM(x.shape, x.dtype) for x in shapes] + [
        pltpu.SemaphoreType.DMA((6,)),
        pltpu.SemaphoreType.DMA((6,)),
        pltpu.SemaphoreType.DMA((14,)),
    ]
    whole = pl.BlockSpec(memory_space=pltpu.HBM)
    made = pl.pallas_call(
        functools.partial(kernel, (groups, regs, zn, rays, segs, samples)),
        out_shape=shapes,
        in_specs=[whole] * 10,
        out_specs=[whole] * 4,
        scratch_shapes=scratch,
        compiler_params=pltpu.CompilerParams(
            collective_id=0, has_side_effects=True, vmem_limit_bytes=VMEM_BYTES
        ),
        name="radiance_step",
    )(*operands)
    colours, g_in, g_hid, g_head = pl.pallas_call(
        hand_over,
        out_shape=shapes,
        in_specs=[whole] * 4,
        out_specs=[whole] * 4,
        scratch_shapes=[pltpu.SemaphoreType.DMA((4,))],
        name="hand_over",
    )(*made)
    return colours, g_in, g_hid, g_head.T[None]


def solution(mesh):
    both = ("grp", "reg")
    return jax.shard_map(
        per_device,
        mesh=mesh,
        in_specs=(
            P(None, both), P(None, both), P(None, both), P(both, None), P(both, None),
            P(both, None, None), P(), P(both, None, None), P(both, None, None, None),
            P(both, None, None),
        ),
        out_specs=(
            P(None, both), P(both, None, None), P(both, None, None, None), P(both, None, None),
        ),
        check_vma=False,
    )
```

```python
import functools
import math

import jax
import jax.numpy as jnp
from jax import lax
from jax.experimental import pallas as pl
from jax.experimental.pallas import tpu as pltpu
from jax.sharding import PartitionSpec as P

DEPTHS = 128
CHIPS_Z = 8
VMEM_BYTES = 64 * 1024 * 1024
LANES = 128
MESH = pl.DeviceIdType.MESH
F32 = jnp.float32
BF16 = jnp.bfloat16

SIN = (6.283182621002197, -41.34142303466797, 81.59620666503906, -76.58030700683594,
       41.2061653137207, -12.272321701049805)
COS = (1.0, -19.73920440673828, 64.93911743164062, -85.45016479492188, 60.16783142089844,
       -25.968313217163086, 6.529609680175781)


def horner(coefficients, x):
    total = jnp.full_like(x, coefficients[-1])
    for value in coefficients[-2::-1]:
        total = total * x + value
    return total


def dot(a, b):
    return jnp.dot(a, b, preferred_element_type=F32)


def dot_nt(a, b):
    return lax.dot_general(a, b, (((1,), (1,)), ((), ())), preferred_element_type=F32)


def pieces(x):
    high = x.astype(BF16).astype(F32)
    rest = x - high
    middle = rest.astype(BF16).astype(F32)
    return high, middle, (rest - middle).astype(BF16).astype(F32)


def exchange(source, target, rows, count, me, device, send, receive):
    def part(ref, index):
        return ref.at[pl.ds(pl.multiple_of(index * rows, rows), rows)]

    for step in range(1, count):
        peer = lax.rem(me + step, count)
        pltpu.make_async_remote_copy(
            src_ref=part(source, peer),
            dst_ref=part(target, me),
            send_sem=send,
            recv_sem=receive,
            device_id=device(peer),
            device_id_type=MESH,
        ).start()
    own = pl.ds(pl.multiple_of(me * rows, rows), rows)
    target[own, :] = source[own, :]
    others = pl.ds(0, (count - 1) * rows)
    everything = pltpu.make_async_remote_copy(
        src_ref=source.at[others],
        dst_ref=target.at[others],
        send_sem=send,
        recv_sem=receive,
        device_id=device(lax.rem(me + 1, count)),
        device_id_type=MESH,
    )
    return everything.wait_recv, everything.wait_send


def direct(source, target, row_of, own_row, slot, where, send, receive):
    groups, side, zn, grp, me_y, me_x, me_z, regs = where

    def ring(index):
        half = index // 2 if isinstance(index, int) else lax.div(index, 2)
        odd = index % 2 if isinstance(index, int) else lax.rem(index, 2)
        return zn // 2 + half - odd * (2 * half + 1)

    def layer(index, nearest):
        z = lax.rem(me_z + ring(index), zn)
        for y, x in sorted(
            ((y, x) for y in range(side) for x in range(side)),
            key=lambda q: -min(q[0], side - q[0]) - min(q[1], side - q[1]),
        ):
            far = lax.rem(me_y + y, side) * side + lax.rem(me_x + x, side)
            for core in range(groups - 1, -1, -1):
                if nearest and y == x == core == 0:
                    continue
                c = lax.rem(grp + core, groups)
                pltpu.make_async_remote_copy(
                    src_ref=source.at[pl.ds(row_of(c, far, z), 1)],
                    dst_ref=target.at[pl.ds(own_row, 1)],
                    send_sem=send,
                    recv_sem=receive,
                    device_id=(c, far * zn + z),
                    device_id_type=MESH,
                ).start()

    def body(index, carry):
        layer(index, False)
        return carry

    lax.fori_loop(0, zn - 1, body, 0)
    layer(zn - 1, True)
    target[pl.ds(own_row, 1), :] = source[pl.ds(slot, 1), :]
    count = groups * regs - 1
    everything = pltpu.make_async_remote_copy(
        src_ref=source.at[pl.ds(0, count)],
        dst_ref=target.at[pl.ds(0, count)],
        send_sem=send,
        recv_sem=receive,
        device_id=(lax.rem(grp + 1, groups), (me_y * side + me_x) * zn + me_z),
        device_id_type=MESH,
    )
    return everything.wait_recv, everything.wait_send


def turned(source, loose, target, major, minor):
    loose[...] = source[...].astype(F32)
    for index in range(minor):
        target[index * major : (index + 1) * major, :] = loose[
            pl.ds(index, major, stride=minor), :
        ].astype(BF16)


def staged(stages, count):
    for step in range(count + stages - 1):
        for stage in range(stages):
            if 0 <= step - stage < count:
                yield stage, step - stage


def kernel(
    sizes,
    *refs,
):
    arguments, results = refs[:10], refs[10:14]
    (
    send1, mid1, turn1, last1, loose, send2, last2, send3, last3, rows_s, words_s, words_b, onehot, freq_s, slots_s, phase0, phase1, depth_s, head_s,
    raw_s, graw_s, cot_b, w1t, w2t, w3t, w2, w3, wot, wo, encoded, hidden, slope, cotangents,
    acc1, acc2, acc3, acc4, colours, g_in, g_hid, g_head, sends, receives, local,
    ) = refs[24:]
    held = refs[14:24]
    anchors, directions, targets, regions, counts, depths, frequencies, w1, wh, w_head = held
    made = (colours, g_in, g_hid, g_head)
    groups, regs, zn, rays, segs, samples = sizes
    loads = [
        pltpu.make_async_copy(argument, place, local.at[index])
        for index, (argument, place) in enumerate(zip(arguments, held))
    ]
    for load in loads:
        load.start()
    n = groups * regs
    near, far = groups * zn, regs // zn
    slots = 2 * n
    width = segs * rays
    side = math.isqrt(far)
    features = wh.shape[-1]
    freqs = features // 2

    grp = lax.axis_index("grp").astype(jnp.int32)
    reg = lax.axis_index("reg").astype(jnp.int32)
    me_far = lax.div(reg, zn)
    me_z = lax.rem(reg, zn)
    me_near = grp * zn + me_z

    def near_device(index):
        return (lax.div(index, zn), me_far * zn + lax.rem(index, zn))

    def far_device(index):
        return (grp, index * zn + me_z)

    where = (groups, side, zn, grp, lax.div(me_far, side), lax.rem(me_far, side), me_z, regs)

    def region_row(c, yx, z):
        return (c * zn + z) * far + yx

    def source_row(c, yx, z):
        return yx * near + c * zn + z

    my_region_row = region_row(grp, me_far, me_z)
    my_source_row = source_row(grp, me_far, me_z)
    barrier = pltpu.get_barrier_semaphore()

    for count, me, device in ((near, me_near, near_device), (far, me_far, far_device)):
        for step in range(1, count):
            pl.semaphore_signal(
                barrier, inc=1, device_id=device(lax.rem(me + step, count)), device_id_type=MESH
            )
    for index in (0, 1, 3, 4, 5):
        loads[index].wait()

    ids = regions[...]
    in_group = lax.rem(ids, regs)
    place = (lax.div(ids, regs) * zn + lax.rem(in_group, zn)) * far + lax.div(in_group, zn)
    rows_s[...] = jnp.full(rows_s.shape, -1, jnp.int32)
    words_s[...] = jnp.zeros(words_s.shape, F32)
    for k in range(segs):
        part = slice(k * rays, (k + 1) * rays)
        rows_s[0:1, part] = place[k : k + 1]
        both = jnp.concatenate([anchors[...], directions[...]], axis=0)
        high, middle, low = pieces(both)
        words_s[0:6, part] = high
        words_s[6:12, part] = middle
        words_s[12:18, part] = low
        words_s[18:19, part] = counts[k : k + 1].astype(F32)
        words_s[24 : 24 + samples, part] = depths[k].astype(F32)
    row_of = rows_s[0:1, :]
    match = row_of == lax.broadcasted_iota(jnp.int32, (n, width), 0)
    number = lax.broadcasted_iota(jnp.int32, (n, width), 1)
    last = jnp.max(jnp.where(match, number, -1), axis=1, keepdims=True)
    first_slot = number == last
    onehot[:, 0:width] = jnp.where(first_slot, 1.0, 0.0).astype(BF16)
    onehot[:, width:] = jnp.where(match & jnp.logical_not(first_slot), 1.0, 0.0).astype(BF16)
    words_b[...] = jnp.zeros(words_b.shape, BF16)
    packed = words_s[...].astype(BF16)
    words_b[0:32, 0:width] = packed
    words_b[32:64, width:] = packed
    send1[...] = dot_nt(onehot[...], words_b[...]).astype(BF16)

    pl.semaphore_wait(barrier, near + far - 2)

    wait_near1, sent_near1 = exchange(
        send1, mid1, far, near, me_near, near_device, sends.at[0], receives.at[0]
    )
    for index in (2, 6, 7, 8, 9):
        loads[index].wait()
    w1t[...] = (w1[0].astype(F32) * 0.5).T.astype(BF16)
    half2 = wh[0, 0].astype(F32) * 0.5
    w2[...] = half2.astype(BF16)
    w2t[...] = half2.T.astype(BF16)
    half3 = wh[0, 1].astype(F32) * 0.5
    w3[...] = half3.astype(BF16)
    w3t[...] = half3.T.astype(BF16)
    wait_near1()
    turned(mid1, loose, turn1, near, far)
    wait_far1, sent_far1 = exchange(
        turn1, last1, near, far, me_far, far_device, sends.at[1], receives.at[1]
    )
    head_s[...] = jnp.zeros(head_s.shape, F32)
    head_s[0:4, :] = w_head[...].astype(F32)
    wot[...] = head_s[...].astype(BF16)
    wo[...] = (head_s[...] * 0.5).T.astype(BF16)
    freq_s[...] = jnp.zeros(freq_s.shape, F32)
    freq_s[0:3, :] = frequencies[...] * (1.0 / (2.0 * math.pi))
    columns = freq_s[...].T
    send2[...] = jnp.zeros(send2.shape, F32)
    send3[...] = jnp.zeros(send3.shape, F32)
    graw_s[...] = jnp.zeros(graw_s.shape, F32)
    cot_b[...] = jnp.zeros(cot_b.shape, BF16)
    wait_far1()

    words = last1[...].astype(F32).T
    slots_s[:, 0:n] = words[0:32]
    slots_s[:, n:] = words[32:64]
    geometry = (slots_s[0:6, :] + slots_s[6:12, :]) + slots_s[12:18, :]
    base = jnp.zeros((freqs, slots), F32)
    rate = jnp.zeros((freqs, slots), F32)
    for c in range(3):
        base = base + columns[:, c : c + 1] * geometry[c : c + 1]
        rate = rate + columns[:, c : c + 1] * geometry[3 + c : 4 + c]
    phase0[...] = base
    phase1[...] = rate
    depth_s[...] = 0.1 + (slots_s[24 : 24 + samples, :] + 0.5) * (2.0 / DEPTHS)
    live = jnp.where(
        lax.broadcasted_iota(jnp.int32, (samples, slots), 0).astype(F32) < slots_s[18:19, :],
        1.0, 0.0,
    )

    layers = (w1t, w2t, w3t)
    for stage, j in staged(5, samples):
        if stage == 0:
            turns = phase0[...] + depth_s[j : j + 1, :] * phase1[...]
            r = turns - jnp.round(turns)
            square = r * r
            encoded[j, 0:freqs] = (r * horner(SIN, square)).astype(BF16)
            encoded[j, freqs:] = horner(COS, square).astype(BF16)
        elif stage < 4:
            z = dot(layers[stage - 1][...], encoded[j] if stage == 1 else hidden[stage - 2, j])
            t = jnp.tanh(z)
            h = z + z * t
            hidden[stage - 1, j] = h.astype(BF16)
            slope[stage - 1, j] = ((1.0 + h) + t * (1.0 - h)).astype(BF16)
        else:
            raw = dot(wot[...], hidden[2, j])
            for k in range(4):
                raw_s[k, j : j + 1, :] = raw[k : k + 1]

    density = raw_s[0]
    small = jnp.exp(-jnp.abs(density))
    softplus = jnp.maximum(density, 0.0) + jnp.log1p(small)
    clear = jnp.exp(-0.5 * softplus)
    alpha = live * (1.0 - clear)
    keep = 1.0 - alpha
    tone = [jax.nn.sigmoid(raw_s[1 + c]) for c in range(3)]
    through = jnp.ones((1, slots), F32)
    befores = []
    for i in range(samples):
        befores.append(through)
        through = through * keep[i : i + 1]
    before = jnp.concatenate(befores, axis=0)
    weight = before * alpha
    seg = [jnp.sum(weight * tone[c], axis=0, keepdims=True) for c in range(3)] + [through]
    answer = jnp.concatenate(seg, axis=0)
    blank = jnp.zeros((4, slots), F32)
    answer = jnp.concatenate(list(pieces(answer)) + [blank], axis=0)
    answer = jnp.concatenate([answer[:, 0:n], answer[:, n:]], axis=0)
    send2[:, 0:32] = answer.T

    wait2, sent2 = direct(
        send2, last2, source_row, my_region_row, my_source_row, where, sends.at[2], receives.at[2]
    )
    d_density = 0.5 * live * clear * jnp.where(density >= 0.0, 1.0, small) / (1.0 + small)
    d_tone = [weight * t * (1.0 - t) for t in tone]
    wait2()

    values = last2[...].T[0:32].astype(BF16)
    found = dot(values[0:16], onehot[:, 0:width]) + dot(values[16:32], onehot[:, width:])
    found = (found[0:4] + found[4:8]) + found[8:12]
    arrive = [jnp.ones((1, rays), F32)]
    total = jnp.zeros((3, rays), F32)
    parts = []
    for k in range(segs):
        part = found[:, k * rays : (k + 1) * rays]
        parts.append(part)
        total = total + arrive[k] * part[0:3]
        arrive.append(arrive[k] * part[3:4])
    total = total + arrive[segs]
    colours[...] = total
    error = total - targets[...]
    behind = jnp.sum(error, axis=0, keepdims=True)
    for k in range(segs - 1, -1, -1):
        part = parts[k]
        cotangent = jnp.concatenate([arrive[k] * error, arrive[k] * behind], axis=0)
        behind = jnp.sum(error * part[0:3], axis=0, keepdims=True) + part[3:4] * behind
        stack = jnp.concatenate(
            list(pieces(cotangent)) + [jnp.zeros((4, rays), F32)], axis=0
        ).astype(BF16)
        cot_b[0:16, k * rays : (k + 1) * rays] = stack
        cot_b[16:32, width + k * rays : width + (k + 1) * rays] = stack
    send3[:, 0:32] = dot_nt(onehot[...], cot_b[...])

    wait3, sent3 = direct(
        send3, last3, region_row, my_source_row, my_region_row, where, sends.at[3], receives.at[3]
    )
    wait3()

    words = last3[...].T[0:32]
    given = jnp.concatenate(
        [(words[0:4] + words[4:8]) + words[8:12], (words[16:20] + words[20:24]) + words[24:28]],
        axis=1,
    )
    gain = given[0:1] * tone[0] + given[1:2] * tone[1] + given[2:3] * tone[2]
    after = given[3:4]
    backs = []
    for i in range(samples - 1, -1, -1):
        backs.append(befores[i] * (gain[i : i + 1] - after))
        after = alpha[i : i + 1] * gain[i : i + 1] + keep[i : i + 1] * after
    d_raw = [jnp.concatenate(backs[::-1], axis=0) * d_density]
    d_raw += [given[c : c + 1] * d_tone[c] for c in range(3)]
    for j in range(samples):
        for k in range(4):
            graw_s[j, k : k + 1, :] = d_raw[k][j : j + 1]

    backs = (wo, w3, w2)
    inputs = (lambda j: hidden[1, j], lambda j: hidden[0, j], lambda j: encoded[j])
    totals = (acc3, acc2, acc1)

    def gather(total, j, term):
        if j == 0:
            total[...] = term
        else:
            total[...] += term

    for stage, j in staged(4, samples):
        if stage == 0:
            gather(acc4, j, dot_nt(graw_s[j].astype(BF16), hidden[2, j]))
        if stage < 3:
            g = graw_s[j].astype(BF16) if stage == 0 else cotangents[stage - 1, j]
            g = dot(backs[stage][...], g) * slope[2 - stage, j].astype(F32)
            cotangents[stage, j] = g.astype(BF16)
        if stage > 0:
            gather(totals[stage - 1], j, dot_nt(inputs[stage - 1](j), cotangents[stage - 1, j]))

    g_in[0] = acc1[...].astype(BF16)
    g_hid[0, 0] = acc2[...].astype(BF16)
    g_hid[0, 1] = acc3[...].astype(BF16)
    g_head[...] = acc4[0:4, :].astype(BF16)
    stores = [
        pltpu.make_async_copy(place, result, local.at[10 + index])
        for index, (place, result) in enumerate(zip(made, results))
    ]
    for store in stores:
        store.start()
    for store in stores:
        store.wait()

    for sent in (sent_near1, sent_far1, sent2, sent3):
        sent()


def hand_over(*refs):
    sources, results, places, sems = refs[:4], refs[4:8], refs[8:12], refs[12]
    loads = [
        pltpu.make_async_copy(sources[index], places[index], sems.at[index]) for index in range(4)
    ]
    stores = [
        pltpu.make_async_copy(places[index], results[index], sems.at[4 + index])
        for index in range(4)
    ]
    for load in loads:
        load.start()
    for load, store in zip(loads, stores):
        load.wait()
        store.start()
    for store in stores:
        store.wait()


def per_device(
    anchors, directions, targets, region_ids, sample_counts, depth_index, frequencies,
    w_input, w_hidden, w_head,
):
    groups, regs = lax.axis_size("grp"), lax.axis_size("reg")
    rays, segs = region_ids.shape
    samples = depth_index.shape[2]
    width = w_input.shape[1]
    zn = min(CHIPS_Z, regs)
    n = groups * regs
    slots = 2 * n
    near, far = groups * zn, regs // zn
    lanes = segs * rays
    board = [pltpu.VMEM((n, LANES), BF16)] * 4 + [pltpu.VMEM((n, LANES), F32)] * 5
    square = (width, width)
    operands = (
        anchors, directions, targets, region_ids.T, sample_counts.T,
        depth_index.transpose(1, 2, 0), frequencies, w_input, w_hidden, w_head[0].T,
    )
    shapes = (
        jax.ShapeDtypeStruct((3, rays), F32),
        jax.ShapeDtypeStruct(w_input.shape, BF16),
        jax.ShapeDtypeStruct(w_hidden.shape, BF16),
        jax.ShapeDtypeStruct((4, width), BF16),
    )
    scratch = [pltpu.VMEM(x.shape, x.dtype) for x in operands] + board + [
        pltpu.VMEM((8, lanes), jnp.int32),
        pltpu.VMEM((32, lanes), F32),
        pltpu.VMEM((LANES, 2 * lanes), BF16),
        pltpu.VMEM((n, 2 * lanes), BF16),
        pltpu.VMEM((8, width // 2), F32),
        pltpu.VMEM((32, slots), F32),
        pltpu.VMEM((width // 2, slots), F32),
        pltpu.VMEM((width // 2, slots), F32),
        pltpu.VMEM((samples, slots), F32),
        pltpu.VMEM((16, width), F32),
        pltpu.VMEM((4, samples, slots), F32),
        pltpu.VMEM((samples, 16, slots), F32),
        pltpu.VMEM((32, 2 * lanes), BF16),
        pltpu.VMEM(square, BF16),
        pltpu.VMEM(square, BF16),
        pltpu.VMEM(square, BF16),
        pltpu.VMEM(square, BF16),
        pltpu.VMEM(square, BF16),
        pltpu.VMEM((16, width), BF16),
        pltpu.VMEM((width, 16), BF16),
        pltpu.VMEM((samples, width, slots), BF16),
        pltpu.VMEM((3, samples, width, slots), BF16),
        pltpu.VMEM((3, samples, width, slots), BF16),
        pltpu.VMEM((3, samples, width, slots), BF16),
        pltpu.VMEM(square, F32),
        pltpu.VMEM(square, F32),
        pltpu.VMEM(square, F32),
        pltpu.VMEM((16, width), F32),
    ] + [pltpu.VMEM(x.shape, x.dtype) for x in shapes] + [
        pltpu.SemaphoreType.DMA((4,)),
        pltpu.SemaphoreType.DMA((4,)),
        pltpu.SemaphoreType.DMA((14,)),
    ]
    whole = pl.BlockSpec(memory_space=pltpu.HBM)
    made = pl.pallas_call(
        functools.partial(kernel, (groups, regs, zn, rays, segs, samples)),
        out_shape=shapes,
        in_specs=[whole] * 10,
        out_specs=[whole] * 4,
        scratch_shapes=scratch,
        compiler_params=pltpu.CompilerParams(
            collective_id=0, has_side_effects=True, vmem_limit_bytes=VMEM_BYTES
        ),
        name="radiance_step",
    )(*operands)
    colours, g_in, g_hid, g_head = pl.pallas_call(
        hand_over,
        out_shape=shapes,
        in_specs=[whole] * 4,
        out_specs=[whole] * 4,
        scratch_shapes=[pltpu.VMEM(x.shape, x.dtype) for x in shapes]
        + [pltpu.SemaphoreType.DMA((8,))],
        name="hand_over",
    )(*made)
    return colours, g_in, g_hid, g_head.T[None]


def solution(mesh):
    both = ("grp", "reg")
    return jax.shard_map(
        per_device,
        mesh=mesh,
        in_specs=(
            P(None, both), P(None, both), P(None, both), P(both, None), P(both, None),
            P(both, None, None), P(), P(both, None, None), P(both, None, None, None),
            P(both, None, None),
        ),
        out_specs=(
            P(None, both), P(both, None, None), P(both, None, None, None), P(both, None, None),
        ),
        check_vma=False,
    )
```

```python
import functools
import math

import jax
import jax.numpy as jnp
from jax import lax
from jax.experimental import pallas as pl
from jax.experimental.pallas import tpu as pltpu
from jax.sharding import PartitionSpec as P

DEPTHS = 128
CHIPS_Z = 8
VMEM_BYTES = 64 * 1024 * 1024
LANES = 128
MESH = pl.DeviceIdType.MESH
F32 = jnp.float32
BF16 = jnp.bfloat16

SIN = (4.442883014678955, -7.308241367340088, 3.6062893867492676, -0.8457654118537903,
       0.10920875519514084)
COS = (1.4142135381698608, -6.978850841522217, 5.7394609451293945, -1.8835630416870117,
       0.31069818139076233)


def horner(coefficients, x):
    total = jnp.full_like(x, coefficients[-1])
    for value in coefficients[-2::-1]:
        total = total * x + value
    return total


def dot(a, b):
    return jnp.dot(a, b, preferred_element_type=F32)


def dot_nt(a, b):
    return lax.dot_general(a, b, (((1,), (1,)), ((), ())), preferred_element_type=F32)


def pieces(x):
    high = x.astype(BF16).astype(F32)
    rest = x - high
    middle = rest.astype(BF16).astype(F32)
    return high, middle, (rest - middle).astype(BF16).astype(F32)


def span(offset, size):
    return min(offset, size - offset)


def farthest_first(first, second):
    offsets = [(a, b) for a in range(first) for b in range(second)]
    return sorted(offsets, key=lambda q: (-span(q[0], first) - span(q[1], second), q))


def ranks(side):
    return {offset: place for place, offset in enumerate(reversed(farthest_first(side, side)))}


class Place:
    def __init__(self, groups, regs, zn):
        self.groups, self.regs, self.zn = groups, regs, zn
        self.side = math.isqrt(regs // zn)
        self.grp = lax.axis_index("grp").astype(jnp.int32)
        reg = lax.axis_index("reg").astype(jnp.int32)
        self.z = lax.rem(reg, zn)
        self.yx = lax.div(reg, zn)
        self.y, self.x = lax.div(self.yx, self.side), lax.rem(self.yx, self.side)
        self.near = self.grp * zn + self.z
        self.rank = ranks(self.side)

    def shifted(self, core=0, y=0, x=0, z=0):
        c = lax.rem(self.grp + core, self.groups) if core else self.grp
        line = lax.rem(self.y + y, self.side) if y else self.y
        row = lax.rem(self.x + x, self.side) if x else self.x
        layer = self.z if isinstance(z, int) and z == 0 else lax.rem(self.z + z, self.zn)
        return c, line * self.side + row, layer

    def device(self, peer):
        return (peer[0], peer[1] * self.zn + peer[2])

    def opposite(self, y, x):
        return self.rank[(-y % self.side, -x % self.side)]

    def near_offsets(self):
        return [(c, z) for c, z in farthest_first(self.groups, self.zn) if (c, z) != (0, 0)]

    def far_offsets(self):
        return [(y, x) for y, x in farthest_first(self.side, self.side) if (y, x) != (0, 0)]


def send_part(source, target, rows, start, end, send, receive, device):
    part = pltpu.make_async_remote_copy(
        src_ref=source.at[pl.ds(start, rows)],
        dst_ref=target.at[pl.ds(end, rows)],
        send_sem=send,
        recv_sem=receive,
        device_id=device,
        device_id_type=MESH,
    )
    part.start()


def bytes_of(source, target, rows, send, receive, device):
    return pltpu.make_async_remote_copy(
        src_ref=source.at[pl.ds(0, rows)],
        dst_ref=target.at[pl.ds(0, rows)],
        send_sem=send,
        recv_sem=receive,
        device_id=device,
        device_id_type=MESH,
    )


def near_exchange(at, source, target, rows, send, receive):
    mine = pl.multiple_of(at.near * rows, rows)
    for core, z in at.near_offsets():
        peer = at.shifted(core=core, z=z)
        start = pl.multiple_of((peer[0] * at.zn + peer[2]) * rows, rows)
        send_part(source, target, rows, start, mine, send, receive, at.device(peer))
    target[pl.ds(mine, rows), :] = source[pl.ds(mine, rows), :]
    others = (at.groups * at.zn - 1) * rows
    return bytes_of(source, target, others, send, receive, at.device(at.shifted(core=1)))


def far_exchange(at, source, target, rows, send, receives):
    count = at.side * at.side
    for y, x in at.far_offsets():
        peer = at.shifted(y=y, x=x)
        start = pl.multiple_of(peer[1] * rows, rows)
        end = at.opposite(y, x)
        receive = receives.at[2 * end // count]
        send_part(source, target, rows, start, end * rows, send, receive, at.device(peer))
    target[0:rows, :] = source[pl.ds(pl.multiple_of(at.yx * rows, rows), rows), :]
    device = at.device(at.shifted(y=1))
    first, second = (count // 2 - 1) * rows, count // 2 * rows
    return (
        bytes_of(source, target, first, send, receives.at[0], device),
        bytes_of(source, target, second, send, receives.at[1], device),
    )


def direct(at, source, target, start_of, end_of, send, receive):
    zn = at.zn

    def ring(index):
        half = index // 2 if isinstance(index, int) else lax.div(index, 2)
        odd = index % 2 if isinstance(index, int) else lax.rem(index, 2)
        return zn // 2 + half - odd * (2 * half + 1)

    def layer(index, nearest):
        for y, x in farthest_first(at.side, at.side):
            for core in range(at.groups - 1, -1, -1):
                if nearest and y == x == core == 0:
                    continue
                peer = at.shifted(core=core, y=y, x=x, z=0 if nearest else ring(index))
                send_part(
                    source, target, 1, start_of(peer, y, x), end_of(y, x), send, receive,
                    at.device(peer),
                )

    def body(index, carry):
        layer(index, False)
        return carry

    lax.fori_loop(0, zn - 1, body, 0)
    layer(zn - 1, True)
    own = source[pl.ds(start_of(at.shifted(), 0, 0), 1), :]
    target[pl.ds(end_of(0, 0), 1), :] = own
    count = at.groups * at.regs - 1
    return bytes_of(source, target, count, send, receive, at.device(at.shifted(core=1)))


def turned(source, loose, target, major, minor):
    loose[...] = source[...].astype(F32)
    for index in range(minor):
        target[index * major : (index + 1) * major, :] = loose[
            pl.ds(index, major, stride=minor), :
        ].astype(BF16)


def staged(stages, count):
    for step in range(count + stages - 1):
        for stage in range(stages):
            if 0 <= step - stage < count:
                yield stage, step - stage


def kernel(
    sizes,
    *refs,
):
    arguments, results = refs[:10], refs[10:14]
    (
    send1, mid1, turn1, last1, loose, send2, last2, send3, last3, rows_s, words_s, words_b, onehot, freq_s, slots_s, phase0, phase1, depth_s, head_s,
    raw_s, graw_s, cot_b, w1t, w2t, w3t, w2, w3, wot, wo, encoded, hidden, slope, cotangents,
    acc1, acc2, acc3, acc4, colours, g_in, g_hid, g_head, sends, receives, local,
    ) = refs[24:]
    held = refs[14:24]
    anchors, directions, targets, regions, counts, depths, frequencies, w1, wh, w_head = held
    made = (colours, g_in, g_hid, g_head)
    groups, regs, zn, rays, segs, samples = sizes
    loads = [
        pltpu.make_async_copy(argument, place, local.at[index])
        for index, (argument, place) in enumerate(zip(arguments, held))
    ]
    for load in loads:
        load.start()
    n = groups * regs
    near, far = groups * zn, regs // zn
    slots = 2 * n
    width = segs * rays
    features = wh.shape[-1]
    freqs = features // 2

    at = Place(groups, regs, zn)

    def region_row(peer, y=0, x=0):
        return (peer[0] * zn + peer[2]) * far + peer[1]

    def source_row(peer, y, x):
        return at.rank[(y, x)] * near + peer[0] * zn + peer[2]

    barrier = pltpu.get_barrier_semaphore()
    greeted = [at.shifted(core=c, z=z) for c, z in at.near_offsets()]
    greeted += [at.shifted(y=y, x=x) for y, x in at.far_offsets()]
    for peer in greeted:
        pl.semaphore_signal(barrier, inc=1, device_id=at.device(peer), device_id_type=MESH)
    for index in (0, 1, 3, 4, 5):
        loads[index].wait()

    ids = regions[...]
    in_group = lax.rem(ids, regs)
    place = (lax.div(ids, regs) * zn + lax.rem(in_group, zn)) * far + lax.div(in_group, zn)
    rows_s[...] = jnp.full(rows_s.shape, -1, jnp.int32)
    words_s[...] = jnp.zeros(words_s.shape, F32)
    for k in range(segs):
        part = slice(k * rays, (k + 1) * rays)
        rows_s[0:1, part] = place[k : k + 1]
        both = jnp.concatenate([anchors[...], directions[...]], axis=0)
        high, middle, low = pieces(both)
        words_s[0:6, part] = high
        words_s[6:12, part] = middle
        words_s[12:18, part] = low
        words_s[18:19, part] = counts[k : k + 1].astype(F32)
        words_s[24 : 24 + samples, part] = depths[k].astype(F32)
    row_of = rows_s[0:1, :]
    match = row_of == lax.broadcasted_iota(jnp.int32, (n, width), 0)
    number = lax.broadcasted_iota(jnp.int32, (n, width), 1)
    last = jnp.max(jnp.where(match, number, -1), axis=1, keepdims=True)
    first_slot = number == last
    onehot[:, 0:width] = jnp.where(first_slot, 1.0, 0.0).astype(BF16)
    onehot[:, width:] = jnp.where(match & jnp.logical_not(first_slot), 1.0, 0.0).astype(BF16)
    words_b[...] = jnp.zeros(words_b.shape, BF16)
    packed = words_s[...].astype(BF16)
    words_b[0:32, 0:width] = packed
    words_b[32:64, width:] = packed
    send1[...] = dot_nt(onehot[...], words_b[...]).astype(BF16)

    pl.semaphore_wait(barrier, near + far - 2)

    near1 = near_exchange(at, send1, mid1, far, sends.at[0], receives.at[0])
    for index in (2, 6, 7, 8, 9):
        loads[index].wait()
    w1t[...] = (w1[0].astype(F32) * 0.5).T.astype(BF16)
    half2 = wh[0, 0].astype(F32) * 0.5
    w2[...] = half2.astype(BF16)
    w2t[...] = half2.T.astype(BF16)
    half3 = wh[0, 1].astype(F32) * 0.5
    w3[...] = half3.astype(BF16)
    w3t[...] = half3.T.astype(BF16)
    near1.wait_recv()
    turned(mid1, loose, turn1, near, far)
    halves = far_exchange(at, turn1, last1, near, sends.at[1], receives.at[pl.ds(1, 2)])
    head_s[...] = jnp.zeros(head_s.shape, F32)
    head_s[0:4, :] = w_head[...].astype(F32)
    wot[...] = head_s[...].astype(BF16)
    wo[...] = (head_s[...] * 0.5).T.astype(BF16)
    freq_s[...] = jnp.zeros(freq_s.shape, F32)
    freq_s[0:3, :] = frequencies[...] * (1.0 / (2.0 * math.pi))
    columns = freq_s[...].T
    send2[...] = jnp.zeros(send2.shape, F32)
    send3[...] = jnp.zeros(send3.shape, F32)
    graw_s[...] = jnp.zeros(graw_s.shape, F32)
    cot_b[...] = jnp.zeros(cot_b.shape, BF16)

    lane = n // 2
    part = 2 * lane

    def decode(half):
        words = last1[half * lane : (half + 1) * lane, :].astype(F32).T
        there = slice(half * part, (half + 1) * part)
        slots_s[:, half * part : half * part + lane] = words[0:32]
        slots_s[:, half * part + lane : (half + 1) * part] = words[32:64]
        geometry = (slots_s[0:6, there] + slots_s[6:12, there]) + slots_s[12:18, there]
        base = jnp.zeros((freqs, part), F32)
        rate = jnp.zeros((freqs, part), F32)
        for c in range(3):
            base = base + columns[:, c : c + 1] * geometry[c : c + 1]
            rate = rate + columns[:, c : c + 1] * geometry[3 + c : 4 + c]
        phase0[:, there] = base
        phase1[:, there] = rate
        depth_s[:, there] = 0.1 + (slots_s[24 : 24 + samples, there] + 0.5) * (2.0 / DEPTHS)

    layers = (w1t, w2t, w3t)
    for stage, item in staged(5, samples):
        half, first = divmod(2 * item, samples)
        there = slice(half * part, (half + 1) * part)
        if stage == 0:
            if first == 0:
                halves[half].wait_recv()
                decode(half)
            for side in range(2):
                turns = phase0[:, there] + depth_s[first + side : first + side + 1, there] * phase1[:, there]
                r = turns - jnp.round(turns)
                square = r * r
                sine = r * horner(SIN, square)
                columns_of = slice(side * part, (side + 1) * part)
                encoded[item, 0:freqs, columns_of] = (sine * horner(COS, square)).astype(BF16)
                encoded[item, freqs:, columns_of] = (1.0 - sine * sine).astype(BF16)
        elif stage < 4:
            z = dot(
                layers[stage - 1][...], encoded[item] if stage == 1 else hidden[stage - 2, item]
            )
            t = jnp.tanh(z)
            hidden[stage - 1, item] = (z + z * t).astype(BF16)
            slope[stage - 1, item] = t.astype(BF16)
        else:
            raw = dot(wot[...], hidden[2, item])
            for side in range(2):
                for k in range(4):
                    raw_s[k, first + side : first + side + 1, there] = raw[
                        k : k + 1, side * part : (side + 1) * part
                    ]

    live = jnp.where(
        lax.broadcasted_iota(jnp.int32, (samples, slots), 0).astype(F32) < slots_s[18:19, :],
        1.0, 0.0,
    )
    density = raw_s[0]
    small = jnp.exp(-jnp.abs(density))
    softplus = jnp.maximum(density, 0.0) + jnp.log1p(small)
    clear = jnp.exp(-0.5 * softplus)
    alpha = live * (1.0 - clear)
    keep = 1.0 - alpha
    tone = [jax.nn.sigmoid(raw_s[1 + c]) for c in range(3)]
    through = jnp.ones((1, slots), F32)
    befores = []
    for i in range(samples):
        befores.append(through)
        through = through * keep[i : i + 1]
    before = jnp.concatenate(befores, axis=0)
    weight = before * alpha
    seg = [jnp.sum(weight * tone[c], axis=0, keepdims=True) for c in range(3)] + [through]
    answer = jnp.concatenate(seg, axis=0)
    blank = jnp.zeros((4, slots), F32)
    answer = jnp.concatenate(list(pieces(answer)) + [blank], axis=0)
    answer = jnp.concatenate(
        [
            jnp.concatenate([answer[:, 0:lane], answer[:, part : part + lane]], axis=1),
            jnp.concatenate([answer[:, lane:part], answer[:, part + lane :]], axis=1),
        ],
        axis=0,
    )
    send2[:, 0:32] = answer.T

    back = direct(
        at, send2, last2, source_row, lambda y, x: region_row(at.shifted()), sends.at[2],
        receives.at[3],
    )

    def slopes(item, carry):
        for index in range(3):
            h = hidden[index, item].astype(F32)
            t = slope[index, item].astype(F32)
            slope[index, item] = ((1.0 + h) + t * (1.0 - h)).astype(BF16)
        return carry

    lax.fori_loop(0, samples, slopes, 0)
    d_density = 0.5 * live * clear * jnp.where(density >= 0.0, 1.0, small) / (1.0 + small)
    d_tone = [weight * t * (1.0 - t) for t in tone]
    back.wait_recv()

    values = last2[...].T[0:32].astype(BF16)
    found = dot(values[0:16], onehot[:, 0:width]) + dot(values[16:32], onehot[:, width:])
    found = (found[0:4] + found[4:8]) + found[8:12]
    arrive = [jnp.ones((1, rays), F32)]
    total = jnp.zeros((3, rays), F32)
    parts = []
    for k in range(segs):
        found_part = found[:, k * rays : (k + 1) * rays]
        parts.append(found_part)
        total = total + arrive[k] * found_part[0:3]
        arrive.append(arrive[k] * found_part[3:4])
    total = total + arrive[segs]
    colours[...] = total
    error = total - targets[...]
    behind = jnp.sum(error, axis=0, keepdims=True)
    for k in range(segs - 1, -1, -1):
        found_part = parts[k]
        cotangent = jnp.concatenate([arrive[k] * error, arrive[k] * behind], axis=0)
        behind = jnp.sum(error * found_part[0:3], axis=0, keepdims=True) + found_part[3:4] * behind
        stack = jnp.concatenate(
            list(pieces(cotangent)) + [jnp.zeros((4, rays), F32)], axis=0
        ).astype(BF16)
        cot_b[0:16, k * rays : (k + 1) * rays] = stack
        cot_b[16:32, width + k * rays : width + (k + 1) * rays] = stack
    send3[:, 0:32] = dot_nt(onehot[...], cot_b[...])

    forth = direct(
        at, send3, last3, region_row, lambda y, x: at.opposite(y, x) * near + at.near,
        sends.at[3], receives.at[4],
    )
    forth.wait_recv()

    words = last3[...].T[0:32]
    given = [
        (words[q : q + 4] + words[q + 4 : q + 8]) + words[q + 8 : q + 12] for q in (0, 16)
    ]
    given = jnp.concatenate(
        [given[0][:, 0:lane], given[1][:, 0:lane], given[0][:, lane:], given[1][:, lane:]], axis=1
    )
    gain = given[0:1] * tone[0] + given[1:2] * tone[1] + given[2:3] * tone[2]
    after = given[3:4]
    backs = []
    for i in range(samples - 1, -1, -1):
        backs.append(befores[i] * (gain[i : i + 1] - after))
        after = alpha[i : i + 1] * gain[i : i + 1] + keep[i : i + 1] * after
    d_raw = [jnp.concatenate(backs[::-1], axis=0) * d_density]
    d_raw += [given[c : c + 1] * d_tone[c] for c in range(3)]
    for item in range(samples):
        half, first = divmod(2 * item, samples)
        for side in range(2):
            for k in range(4):
                graw_s[item, k : k + 1, side * part : (side + 1) * part] = d_raw[k][
                    first + side : first + side + 1, half * part : (half + 1) * part
                ]

    stores = [
        pltpu.make_async_copy(place, result, local.at[10 + index])
        for index, (place, result) in enumerate(zip(made, results))
    ]
    stores[0].start()
    backs = (wo, w3, w2)
    inputs = (lambda j: hidden[1, j], lambda j: hidden[0, j], lambda j: encoded[j])
    totals = (acc3, acc2, acc1)

    def gather(total, j, term):
        if j == 0:
            total[...] = term
        else:
            total[...] += term

    ends = (
        (3, g_head, lambda: acc4[0:4, :]),
        (2, g_hid.at[0, 1], lambda: acc3[...]),
        (2, g_hid.at[0, 0], lambda: acc2[...]),
        (1, g_in.at[0], lambda: acc1[...]),
    )
    for stage, j in staged(4, samples):
        if stage == 0:
            gather(acc4, j, dot_nt(graw_s[j].astype(BF16), hidden[2, j]))
        if stage < 3:
            g = graw_s[j].astype(BF16) if stage == 0 else cotangents[stage - 1, j]
            g = dot(backs[stage][...], g) * slope[2 - stage, j].astype(F32)
            cotangents[stage, j] = g.astype(BF16)
        if stage > 0:
            gather(totals[stage - 1], j, dot_nt(inputs[stage - 1](j), cotangents[stage - 1, j]))
        if j == samples - 1:
            index, place, value = ends[stage]
            place[...] = value().astype(BF16)
            if stage != 1:
                stores[index].start()

    for sent in (near1, *halves, back, forth):
        sent.wait_send()
    for store in stores:
        store.wait()


def hand_over(*refs):
    sources, results, places, sems = refs[:4], refs[4:8], refs[8:12], refs[12]
    loads = [
        pltpu.make_async_copy(sources[index], places[index], sems.at[index]) for index in range(4)
    ]
    stores = [
        pltpu.make_async_copy(places[index], results[index], sems.at[4 + index])
        for index in range(4)
    ]
    for load in loads:
        load.start()
    for load, store in zip(loads, stores):
        load.wait()
        store.start()
    for store in stores:
        store.wait()


def per_device(
    anchors, directions, targets, region_ids, sample_counts, depth_index, frequencies,
    w_input, w_hidden, w_head,
):
    groups, regs = lax.axis_size("grp"), lax.axis_size("reg")
    rays, segs = region_ids.shape
    samples = depth_index.shape[2]
    width = w_input.shape[1]
    zn = min(CHIPS_Z, regs)
    n = groups * regs
    slots = 2 * n
    near, far = groups * zn, regs // zn
    lanes = segs * rays
    board = [pltpu.VMEM((n, LANES), BF16)] * 4 + [pltpu.VMEM((n, LANES), F32)] * 5
    square = (width, width)
    operands = (
        anchors, directions, targets, region_ids.T, sample_counts.T,
        depth_index.transpose(1, 2, 0), frequencies, w_input, w_hidden, w_head[0].T,
    )
    shapes = (
        jax.ShapeDtypeStruct((3, rays), F32),
        jax.ShapeDtypeStruct(w_input.shape, BF16),
        jax.ShapeDtypeStruct(w_hidden.shape, BF16),
        jax.ShapeDtypeStruct((4, width), BF16),
    )
    scratch = [pltpu.VMEM(x.shape, x.dtype) for x in operands] + board + [
        pltpu.VMEM((8, lanes), jnp.int32),
        pltpu.VMEM((32, lanes), F32),
        pltpu.VMEM((LANES, 2 * lanes), BF16),
        pltpu.VMEM((n, 2 * lanes), BF16),
        pltpu.VMEM((8, width // 2), F32),
        pltpu.VMEM((32, slots), F32),
        pltpu.VMEM((width // 2, slots), F32),
        pltpu.VMEM((width // 2, slots), F32),
        pltpu.VMEM((samples, slots), F32),
        pltpu.VMEM((16, width), F32),
        pltpu.VMEM((4, samples, slots), F32),
        pltpu.VMEM((samples, 16, slots), F32),
        pltpu.VMEM((32, 2 * lanes), BF16),
        pltpu.VMEM(square, BF16),
        pltpu.VMEM(square, BF16),
        pltpu.VMEM(square, BF16),
        pltpu.VMEM(square, BF16),
        pltpu.VMEM(square, BF16),
        pltpu.VMEM((16, width), BF16),
        pltpu.VMEM((width, 16), BF16),
        pltpu.VMEM((samples, width, slots), BF16),
        pltpu.VMEM((3, samples, width, slots), BF16),
        pltpu.VMEM((3, samples, width, slots), BF16),
        pltpu.VMEM((3, samples, width, slots), BF16),
        pltpu.VMEM(square, F32),
        pltpu.VMEM(square, F32),
        pltpu.VMEM(square, F32),
        pltpu.VMEM((16, width), F32),
    ] + [pltpu.VMEM(x.shape, x.dtype) for x in shapes] + [
        pltpu.SemaphoreType.DMA((4,)),
        pltpu.SemaphoreType.DMA((5,)),
        pltpu.SemaphoreType.DMA((14,)),
    ]
    whole = pl.BlockSpec(memory_space=pltpu.HBM)
    made = pl.pallas_call(
        functools.partial(kernel, (groups, regs, zn, rays, segs, samples)),
        out_shape=shapes,
        in_specs=[whole] * 10,
        out_specs=[whole] * 4,
        scratch_shapes=scratch,
        compiler_params=pltpu.CompilerParams(
            collective_id=0, has_side_effects=True, vmem_limit_bytes=VMEM_BYTES
        ),
        name="radiance_step",
    )(*operands)
    colours, g_in, g_hid, g_head = pl.pallas_call(
        hand_over,
        out_shape=shapes,
        in_specs=[whole] * 4,
        out_specs=[whole] * 4,
        scratch_shapes=[pltpu.VMEM(x.shape, x.dtype) for x in shapes]
        + [pltpu.SemaphoreType.DMA((8,))],
        name="hand_over",
    )(*made)
    return colours, g_in, g_hid, g_head.T[None]


def solution(mesh):
    both = ("grp", "reg")
    return jax.shard_map(
        per_device,
        mesh=mesh,
        in_specs=(
            P(None, both), P(None, both), P(None, both), P(both, None), P(both, None),
            P(both, None, None), P(), P(both, None, None), P(both, None, None, None),
            P(both, None, None),
        ),
        out_specs=(
            P(None, both), P(both, None, None), P(both, None, None, None), P(both, None, None),
        ),
        check_vma=False,
    )
```

```python
import functools
import math

import jax
import jax.numpy as jnp
from jax import lax
from jax.experimental import pallas as pl
from jax.experimental.pallas import tpu as pltpu
from jax.sharding import PartitionSpec as P

DEPTHS = 128
CHIPS_Z = 8
VMEM_BYTES = 64 * 1024 * 1024
LANES = 128
MESH = pl.DeviceIdType.MESH
F32 = jnp.float32
BF16 = jnp.bfloat16

SIN = (4.442883014678955, -7.308241367340088, 3.6062893867492676, -0.8457654118537903,
       0.10920875519514084)
COS = (1.4142135381698608, -6.978850841522217, 5.7394609451293945, -1.8835630416870117,
       0.31069818139076233)


def horner(coefficients, x):
    total = jnp.full_like(x, coefficients[-1])
    for value in coefficients[-2::-1]:
        total = total * x + value
    return total


def dot(a, b):
    return jnp.dot(a, b, preferred_element_type=F32)


def dot_nt(a, b):
    return lax.dot_general(a, b, (((1,), (1,)), ((), ())), preferred_element_type=F32)


def pieces(x):
    high = x.astype(BF16).astype(F32)
    rest = x - high
    middle = rest.astype(BF16).astype(F32)
    return high, middle, (rest - middle).astype(BF16).astype(F32)


def span(offset, size):
    return min(offset, size - offset)


def farthest_first(first, second):
    offsets = [(a, b) for a in range(first) for b in range(second)]
    return sorted(offsets, key=lambda q: (-span(q[0], first) - span(q[1], second), q))


def ranks(side):
    return {offset: place for place, offset in enumerate(reversed(farthest_first(side, side)))}


class Place:
    def __init__(self, groups, regs, zn):
        self.groups, self.regs, self.zn = groups, regs, zn
        self.side = math.isqrt(regs // zn)
        self.grp = lax.axis_index("grp").astype(jnp.int32)
        reg = lax.axis_index("reg").astype(jnp.int32)
        self.z = lax.rem(reg, zn)
        self.yx = lax.div(reg, zn)
        self.y, self.x = lax.div(self.yx, self.side), lax.rem(self.yx, self.side)
        self.near = self.grp * zn + self.z
        self.rank = ranks(self.side)

        def turns(mine, size):
            return [mine] + [lax.rem(mine + step, size) for step in range(1, size)]

        self.cores = turns(self.grp, groups)
        self.layers = turns(self.z, zn)
        ys, xs = turns(self.y, self.side), turns(self.x, self.side)
        self.lines = {
            (y, x): ys[y] * self.side + xs[x] for y in range(self.side) for x in range(self.side)
        }

    def shifted(self, core=0, y=0, x=0, z=0):
        return self.cores[core], self.lines[(y, x)], self.layers[z]

    def device(self, peer):
        return (peer[0], peer[1] * self.zn + peer[2])

    def opposite(self, y, x):
        return self.rank[(-y % self.side, -x % self.side)]

    def near_offsets(self):
        return [(c, z) for c, z in farthest_first(self.groups, self.zn) if (c, z) != (0, 0)]

    def far_offsets(self):
        return [(y, x) for y, x in farthest_first(self.side, self.side) if (y, x) != (0, 0)]


def send_part(source, target, rows, start, end, send, receive, device):
    part = pltpu.make_async_remote_copy(
        src_ref=source.at[pl.ds(start, rows)],
        dst_ref=target.at[pl.ds(end, rows)],
        send_sem=send,
        recv_sem=receive,
        device_id=device,
        device_id_type=MESH,
    )
    part.start()


def bytes_of(source, target, rows, send, receive, device):
    return pltpu.make_async_remote_copy(
        src_ref=source.at[pl.ds(0, rows)],
        dst_ref=target.at[pl.ds(0, rows)],
        send_sem=send,
        recv_sem=receive,
        device_id=device,
        device_id_type=MESH,
    )


def near_exchange(at, source, target, rows, send, receive):
    mine = pl.multiple_of(at.near * rows, rows)
    for core, z in at.near_offsets():
        peer = at.shifted(core=core, z=z)
        start = pl.multiple_of((peer[0] * at.zn + peer[2]) * rows, rows)
        send_part(source, target, rows, start, mine, send, receive, at.device(peer))
    target[pl.ds(mine, rows), :] = source[pl.ds(mine, rows), :]
    others = (at.groups * at.zn - 1) * rows
    return bytes_of(source, target, others, send, receive, at.device(at.shifted(core=1)))


def far_exchange(at, source, target, rows, send, receives):
    count = at.side * at.side
    for y, x in at.far_offsets():
        peer = at.shifted(y=y, x=x)
        start = pl.multiple_of(peer[1] * rows, rows)
        end = at.opposite(y, x)
        receive = receives.at[2 * end // count]
        send_part(source, target, rows, start, end * rows, send, receive, at.device(peer))
    target[0:rows, :] = source[pl.ds(pl.multiple_of(at.yx * rows, rows), rows), :]
    device = at.device(at.shifted(y=1))
    first, second = (count // 2 - 1) * rows, count // 2 * rows
    return (
        bytes_of(source, target, first, send, receives.at[0], device),
        bytes_of(source, target, second, send, receives.at[1], device),
    )


def direct(at, source, target, start, end_of, send, receive):
    zn, lines = at.zn, farthest_first(at.side, at.side)
    devices = {offset: at.lines[offset] * zn for offset in lines}
    starts = {offset: start[2](*offset) for offset in lines}
    ends = {offset: end_of(*offset) for offset in lines}
    of_core = [core * start[0] for core in at.cores]

    def layer(z, nearest):
        bases = [base + z * start[1] for base in of_core]
        for offset in lines:
            for core in range(at.groups - 1, -1, -1):
                if nearest and offset == (0, 0) and core == 0:
                    continue
                send_part(
                    source, target, 1, bases[core] + starts[offset], ends[offset], send, receive,
                    (at.cores[core], devices[offset] + z),
                )

    def body(index, carry):
        half, odd = lax.div(index, 2), lax.rem(index, 2)
        ring = zn // 2 + half - odd * (2 * half + 1)
        layer(lax.rem(at.z + ring, zn), False)
        return carry

    lax.fori_loop(0, zn - 1, body, 0)
    layer(at.z, True)
    own = of_core[0] + at.z * start[1] + starts[(0, 0)]
    target[pl.ds(ends[(0, 0)], 1), :] = source[pl.ds(own, 1), :]
    count = at.groups * at.regs - 1
    return bytes_of(source, target, count, send, receive, at.device(at.shifted(core=1)))


def turned(source, loose, target, major, minor):
    loose[...] = source[...].astype(F32)
    for index in range(minor):
        target[index * major : (index + 1) * major, :] = loose[
            pl.ds(index, major, stride=minor), :
        ].astype(BF16)


def staged(stages, count):
    for step in range(count + stages - 1):
        for stage in range(stages):
            if 0 <= step - stage < count:
                yield stage, step - stage


def kernel(
    sizes,
    *refs,
):
    arguments, results = refs[:10], refs[10:14]
    (
    send1, mid1, turn1, last1, loose, send2, last2, send3, last3, rows_s, words_s, words_b, onehot, freq_s, slots_s, phase0, phase1, depth_s, head_s,
    raw_s, graw_s, cot_b, w1t, w2t, w3t, w2, w3, wot, wo, encoded, hidden, slope, cotangents,
    acc1, acc2, acc3, acc4, colours, g_in, g_hid, g_head, sends, receives, local,
    ) = refs[24:]
    held = refs[14:24]
    anchors, directions, targets, regions, counts, depths, frequencies, w1, wh, w_head = held
    made = (colours, g_in, g_hid, g_head)
    groups, regs, zn, rays, segs, samples = sizes
    loads = [
        pltpu.make_async_copy(argument, place, local.at[index])
        for index, (argument, place) in enumerate(zip(arguments, held))
    ]
    for load in loads:
        load.start()
    n = groups * regs
    near, far = groups * zn, regs // zn
    slots = 2 * n
    width = segs * rays
    features = wh.shape[-1]
    freqs = features // 2

    at = Place(groups, regs, zn)

    region_row = (zn * far, far, lambda y, x: at.lines[(y, x)])
    source_row = (zn, 1, lambda y, x: at.rank[(y, x)] * near)
    my_region_row = at.near * far + at.yx
    barrier = pltpu.get_barrier_semaphore()
    greeted = [at.shifted(core=c, z=z) for c, z in at.near_offsets()]
    greeted += [at.shifted(y=y, x=x) for y, x in at.far_offsets()]
    for peer in greeted:
        pl.semaphore_signal(barrier, inc=1, device_id=at.device(peer), device_id_type=MESH)
    for index in (0, 1, 3, 4, 5):
        loads[index].wait()

    ids = regions[...]
    in_group = lax.rem(ids, regs)
    place = (lax.div(ids, regs) * zn + lax.rem(in_group, zn)) * far + lax.div(in_group, zn)
    rows_s[...] = jnp.full(rows_s.shape, -1, jnp.int32)
    words_s[...] = jnp.zeros(words_s.shape, F32)
    for k in range(segs):
        part = slice(k * rays, (k + 1) * rays)
        rows_s[0:1, part] = place[k : k + 1]
        both = jnp.concatenate([anchors[...], directions[...]], axis=0)
        high, middle, low = pieces(both)
        words_s[0:6, part] = high
        words_s[6:12, part] = middle
        words_s[12:18, part] = low
        words_s[18:19, part] = counts[k : k + 1].astype(F32)
        words_s[24 : 24 + samples, part] = depths[k].astype(F32)
    row_of = rows_s[0:1, :]
    match = row_of == lax.broadcasted_iota(jnp.int32, (n, width), 0)
    number = lax.broadcasted_iota(jnp.int32, (n, width), 1)
    last = jnp.max(jnp.where(match, number, -1), axis=1, keepdims=True)
    first_slot = number == last
    onehot[:, 0:width] = jnp.where(first_slot, 1.0, 0.0).astype(BF16)
    onehot[:, width:] = jnp.where(match & jnp.logical_not(first_slot), 1.0, 0.0).astype(BF16)
    words_b[...] = jnp.zeros(words_b.shape, BF16)
    packed = words_s[...].astype(BF16)
    words_b[0:32, 0:width] = packed
    words_b[32:64, width:] = packed
    send1[...] = dot_nt(onehot[...], words_b[...]).astype(BF16)

    pl.semaphore_wait(barrier, near + far - 2)

    near1 = near_exchange(at, send1, mid1, far, sends.at[0], receives.at[0])
    for index in (2, 6, 7, 8, 9):
        loads[index].wait()
    w1t[...] = (w1[0].astype(F32) * 0.5).T.astype(BF16)
    half2 = wh[0, 0].astype(F32) * 0.5
    w2[...] = half2.astype(BF16)
    w2t[...] = half2.T.astype(BF16)
    half3 = wh[0, 1].astype(F32) * 0.5
    w3[...] = half3.astype(BF16)
    w3t[...] = half3.T.astype(BF16)
    near1.wait_recv()
    turned(mid1, loose, turn1, near, far)
    halves = far_exchange(at, turn1, last1, near, sends.at[1], receives.at[pl.ds(1, 2)])
    head_s[...] = jnp.zeros(head_s.shape, F32)
    head_s[0:4, :] = w_head[...].astype(F32)
    wot[...] = head_s[...].astype(BF16)
    wo[...] = (head_s[...] * 0.5).T.astype(BF16)
    freq_s[...] = jnp.zeros(freq_s.shape, F32)
    freq_s[0:3, :] = frequencies[...] * (1.0 / (2.0 * math.pi))
    columns = freq_s[...].T
    send2[...] = jnp.zeros(send2.shape, F32)
    send3[...] = jnp.zeros(send3.shape, F32)
    graw_s[...] = jnp.zeros(graw_s.shape, F32)
    cot_b[...] = jnp.zeros(cot_b.shape, BF16)

    lane = n // 2
    part = 2 * lane

    def decode(half):
        words = last1[half * lane : (half + 1) * lane, :].astype(F32).T
        there = slice(half * part, (half + 1) * part)
        slots_s[:, half * part : half * part + lane] = words[0:32]
        slots_s[:, half * part + lane : (half + 1) * part] = words[32:64]
        geometry = (slots_s[0:6, there] + slots_s[6:12, there]) + slots_s[12:18, there]
        base = jnp.zeros((freqs, part), F32)
        rate = jnp.zeros((freqs, part), F32)
        for c in range(3):
            base = base + columns[:, c : c + 1] * geometry[c : c + 1]
            rate = rate + columns[:, c : c + 1] * geometry[3 + c : 4 + c]
        phase0[:, there] = base
        phase1[:, there] = rate
        depth_s[:, there] = 0.1 + (slots_s[24 : 24 + samples, there] + 0.5) * (2.0 / DEPTHS)

    layers = (w1t, w2t, w3t)
    for stage, item in staged(5, samples):
        half, first = divmod(2 * item, samples)
        there = slice(half * part, (half + 1) * part)
        if stage == 0:
            if first == 0:
                halves[half].wait_recv()
                decode(half)
            for side in range(2):
                turns = phase0[:, there] + depth_s[first + side : first + side + 1, there] * phase1[:, there]
                r = turns - jnp.round(turns)
                square = r * r
                sine = r * horner(SIN, square)
                columns_of = slice(side * part, (side + 1) * part)
                encoded[item, 0:freqs, columns_of] = (sine * horner(COS, square)).astype(BF16)
                encoded[item, freqs:, columns_of] = (1.0 - sine * sine).astype(BF16)
        elif stage < 4:
            z = dot(
                layers[stage - 1][...], encoded[item] if stage == 1 else hidden[stage - 2, item]
            )
            t = jnp.tanh(z)
            hidden[stage - 1, item] = (z + z * t).astype(BF16)
            slope[stage - 1, item] = t.astype(BF16)
        else:
            raw = dot(wot[...], hidden[2, item])
            for side in range(2):
                for k in range(4):
                    raw_s[k, first + side : first + side + 1, there] = raw[
                        k : k + 1, side * part : (side + 1) * part
                    ]

    live = jnp.where(
        lax.broadcasted_iota(jnp.int32, (samples, slots), 0).astype(F32) < slots_s[18:19, :],
        1.0, 0.0,
    )
    density = raw_s[0]
    small = jnp.exp(-jnp.abs(density))
    softplus = jnp.maximum(density, 0.0) + jnp.log1p(small)
    clear = jnp.exp(-0.5 * softplus)
    alpha = live * (1.0 - clear)
    keep = 1.0 - alpha
    tone = [jax.nn.sigmoid(raw_s[1 + c]) for c in range(3)]
    through = jnp.ones((1, slots), F32)
    befores = []
    for i in range(samples):
        befores.append(through)
        through = through * keep[i : i + 1]
    before = jnp.concatenate(befores, axis=0)
    weight = before * alpha
    seg = [jnp.sum(weight * tone[c], axis=0, keepdims=True) for c in range(3)] + [through]
    answer = jnp.concatenate(seg, axis=0)
    blank = jnp.zeros((4, slots), F32)
    answer = jnp.concatenate(list(pieces(answer)) + [blank], axis=0)
    answer = jnp.concatenate(
        [
            jnp.concatenate([answer[:, 0:lane], answer[:, part : part + lane]], axis=1),
            jnp.concatenate([answer[:, lane:part], answer[:, part + lane :]], axis=1),
        ],
        axis=0,
    )
    send2[:, 0:32] = answer.T

    back = direct(
        at, send2, last2, source_row, lambda y, x: my_region_row, sends.at[2], receives.at[3]
    )

    def slopes(item, carry):
        for index in range(3):
            h = hidden[index, item].astype(F32)
            t = slope[index, item].astype(F32)
            slope[index, item] = ((1.0 + h) + t * (1.0 - h)).astype(BF16)
        return carry

    lax.fori_loop(0, samples, slopes, 0)
    d_density = 0.5 * live * clear * jnp.where(density >= 0.0, 1.0, small) / (1.0 + small)
    d_tone = [weight * t * (1.0 - t) for t in tone]
    back.wait_recv()

    values = last2[...].T[0:32].astype(BF16)
    found = dot(values[0:16], onehot[:, 0:width]) + dot(values[16:32], onehot[:, width:])
    found = (found[0:4] + found[4:8]) + found[8:12]
    arrive = [jnp.ones((1, rays), F32)]
    total = jnp.zeros((3, rays), F32)
    parts = []
    for k in range(segs):
        found_part = found[:, k * rays : (k + 1) * rays]
        parts.append(found_part)
        total = total + arrive[k] * found_part[0:3]
        arrive.append(arrive[k] * found_part[3:4])
    total = total + arrive[segs]
    colours[...] = total
    error = total - targets[...]
    behind = jnp.sum(error, axis=0, keepdims=True)
    for k in range(segs - 1, -1, -1):
        found_part = parts[k]
        cotangent = jnp.concatenate([arrive[k] * error, arrive[k] * behind], axis=0)
        behind = jnp.sum(error * found_part[0:3], axis=0, keepdims=True) + found_part[3:4] * behind
        stack = jnp.concatenate(
            list(pieces(cotangent)) + [jnp.zeros((4, rays), F32)], axis=0
        ).astype(BF16)
        cot_b[0:16, k * rays : (k + 1) * rays] = stack
        cot_b[16:32, width + k * rays : width + (k + 1) * rays] = stack
    send3[:, 0:32] = dot_nt(onehot[...], cot_b[...])

    forth = direct(
        at, send3, last3, region_row, lambda y, x: at.opposite(y, x) * near + at.near,
        sends.at[3], receives.at[4],
    )
    forth.wait_recv()

    words = last3[...].T[0:32]
    given = [
        (words[q : q + 4] + words[q + 4 : q + 8]) + words[q + 8 : q + 12] for q in (0, 16)
    ]
    given = jnp.concatenate(
        [given[0][:, 0:lane], given[1][:, 0:lane], given[0][:, lane:], given[1][:, lane:]], axis=1
    )
    gain = given[0:1] * tone[0] + given[1:2] * tone[1] + given[2:3] * tone[2]
    after = given[3:4]
    backs = []
    for i in range(samples - 1, -1, -1):
        backs.append(befores[i] * (gain[i : i + 1] - after))
        after = alpha[i : i + 1] * gain[i : i + 1] + keep[i : i + 1] * after
    d_raw = [jnp.concatenate(backs[::-1], axis=0) * d_density]
    d_raw += [given[c : c + 1] * d_tone[c] for c in range(3)]
    for item in range(samples):
        half, first = divmod(2 * item, samples)
        for side in range(2):
            for k in range(4):
                graw_s[item, k : k + 1, side * part : (side + 1) * part] = d_raw[k][
                    first + side : first + side + 1, half * part : (half + 1) * part
                ]

    stores = [
        pltpu.make_async_copy(place, result, local.at[10 + index])
        for index, (place, result) in enumerate(zip(made, results))
    ]
    stores[0].start()
    backs = (wo, w3, w2)
    inputs = (lambda j: hidden[1, j], lambda j: hidden[0, j], lambda j: encoded[j])
    totals = (acc3, acc2, acc1)

    def gather(total, j, term):
        if j == 0:
            total[...] = term
        else:
            total[...] += term

    ends = (
        (3, g_head, lambda: acc4[0:4, :]),
        (2, g_hid.at[0, 1], lambda: acc3[...]),
        (2, g_hid.at[0, 0], lambda: acc2[...]),
        (1, g_in.at[0], lambda: acc1[...]),
    )
    for stage, j in staged(4, samples):
        if stage == 0:
            gather(acc4, j, dot_nt(graw_s[j].astype(BF16), hidden[2, j]))
        if stage < 3:
            g = graw_s[j].astype(BF16) if stage == 0 else cotangents[stage - 1, j]
            g = dot(backs[stage][...], g) * slope[2 - stage, j].astype(F32)
            cotangents[stage, j] = g.astype(BF16)
        if stage > 0:
            gather(totals[stage - 1], j, dot_nt(inputs[stage - 1](j), cotangents[stage - 1, j]))
        if j == samples - 1:
            index, place, value = ends[stage]
            place[...] = value().astype(BF16)
            if stage != 1:
                stores[index].start()

    for sent in (near1, *halves, back, forth):
        sent.wait_send()
    for store in stores:
        store.wait()


def hand_over(*refs):
    sources, results, places, sems = refs[:4], refs[4:8], refs[8:12], refs[12]
    width = sources[1].shape[1]
    half = width // 2
    pieces_of = [(0, ()), (3, ())]
    pieces_of += [(2, (0, k, pl.ds(h, half))) for k in range(2) for h in (0, half)]
    pieces_of += [(1, (0, pl.ds(h, half))) for h in (0, half)]

    def part(group, index, where):
        return group[index].at[where] if where else group[index]

    moves = [
        tuple(
            pltpu.make_async_copy(part(a, index, where), part(b, index, where), sems.at[row, number])
            for row, (a, b) in enumerate(((sources, places), (places, results)))
        )
        for number, (index, where) in enumerate(pieces_of)
    ]
    for load, _ in moves:
        load.start()
    for load, store in moves:
        load.wait()
        store.start()
    for _, store in moves:
        store.wait()


def per_device(
    anchors, directions, targets, region_ids, sample_counts, depth_index, frequencies,
    w_input, w_hidden, w_head,
):
    groups, regs = lax.axis_size("grp"), lax.axis_size("reg")
    rays, segs = region_ids.shape
    samples = depth_index.shape[2]
    width = w_input.shape[1]
    zn = min(CHIPS_Z, regs)
    n = groups * regs
    slots = 2 * n
    near, far = groups * zn, regs // zn
    lanes = segs * rays
    board = [pltpu.VMEM((n, LANES), BF16)] * 4 + [pltpu.VMEM((n, LANES), F32)] * 5
    square = (width, width)
    operands = (
        anchors, directions, targets, region_ids.T, sample_counts.T,
        depth_index.transpose(1, 2, 0), frequencies, w_input, w_hidden, w_head[0].T,
    )
    shapes = (
        jax.ShapeDtypeStruct((3, rays), F32),
        jax.ShapeDtypeStruct(w_input.shape, BF16),
        jax.ShapeDtypeStruct(w_hidden.shape, BF16),
        jax.ShapeDtypeStruct((4, width), BF16),
    )
    scratch = [pltpu.VMEM(x.shape, x.dtype) for x in operands] + board + [
        pltpu.VMEM((8, lanes), jnp.int32),
        pltpu.VMEM((32, lanes), F32),
        pltpu.VMEM((LANES, 2 * lanes), BF16),
        pltpu.VMEM((n, 2 * lanes), BF16),
        pltpu.VMEM((8, width // 2), F32),
        pltpu.VMEM((32, slots), F32),
        pltpu.VMEM((width // 2, slots), F32),
        pltpu.VMEM((width // 2, slots), F32),
        pltpu.VMEM((samples, slots), F32),
        pltpu.VMEM((16, width), F32),
        pltpu.VMEM((4, samples, slots), F32),
        pltpu.VMEM((samples, 16, slots), F32),
        pltpu.VMEM((32, 2 * lanes), BF16),
        pltpu.VMEM(square, BF16),
        pltpu.VMEM(square, BF16),
        pltpu.VMEM(square, BF16),
        pltpu.VMEM(square, BF16),
        pltpu.VMEM(square, BF16),
        pltpu.VMEM((16, width), BF16),
        pltpu.VMEM((width, 16), BF16),
        pltpu.VMEM((samples, width, slots), BF16),
        pltpu.VMEM((3, samples, width, slots), BF16),
        pltpu.VMEM((3, samples, width, slots), BF16),
        pltpu.VMEM((3, samples, width, slots), BF16),
        pltpu.VMEM(square, F32),
        pltpu.VMEM(square, F32),
        pltpu.VMEM(square, F32),
        pltpu.VMEM((16, width), F32),
    ] + [pltpu.VMEM(x.shape, x.dtype) for x in shapes] + [
        pltpu.SemaphoreType.DMA((4,)),
        pltpu.SemaphoreType.DMA((5,)),
        pltpu.SemaphoreType.DMA((14,)),
    ]
    whole = pl.BlockSpec(memory_space=pltpu.HBM)
    made = pl.pallas_call(
        functools.partial(kernel, (groups, regs, zn, rays, segs, samples)),
        out_shape=shapes,
        in_specs=[whole] * 10,
        out_specs=[whole] * 4,
        scratch_shapes=scratch,
        compiler_params=pltpu.CompilerParams(
            collective_id=0, has_side_effects=True, vmem_limit_bytes=VMEM_BYTES
        ),
        name="radiance_step",
    )(*operands)
    colours, g_in, g_hid, g_head = pl.pallas_call(
        hand_over,
        out_shape=shapes,
        in_specs=[whole] * 4,
        out_specs=[whole] * 4,
        scratch_shapes=[pltpu.VMEM(x.shape, x.dtype) for x in shapes]
        + [pltpu.SemaphoreType.DMA((2, 8))],
        name="hand_over",
    )(*made)
    return colours, g_in, g_hid, g_head.T[None]


def solution(mesh):
    both = ("grp", "reg")
    return jax.shard_map(
        per_device,
        mesh=mesh,
        in_specs=(
            P(None, both), P(None, both), P(None, both), P(both, None), P(both, None),
            P(both, None, None), P(), P(both, None, None), P(both, None, None, None),
            P(both, None, None),
        ),
        out_specs=(
            P(None, both), P(both, None, None), P(both, None, None, None), P(both, None, None),
        ),
        check_vma=False,
    )
```

```python
import functools
import math

import jax
import jax.numpy as jnp
from jax import lax
from jax.experimental import pallas as pl
from jax.experimental.pallas import tpu as pltpu
from jax.sharding import PartitionSpec as P

DEPTHS = 128
CHIPS_Z = 8
VMEM_BYTES = 64 * 1024 * 1024
LANES = 128
MESH = pl.DeviceIdType.MESH
F32 = jnp.float32
BF16 = jnp.bfloat16

SIN = (4.442883014678955, -7.308241367340088, 3.6062893867492676, -0.8457654118537903,
       0.10920875519514084)
COS = (1.4142135381698608, -6.978850841522217, 5.7394609451293945, -1.8835630416870117,
       0.31069818139076233)


def horner(coefficients, x):
    total = jnp.full_like(x, coefficients[-1])
    for value in coefficients[-2::-1]:
        total = total * x + value
    return total


def dot(a, b):
    return jnp.dot(a, b, preferred_element_type=F32)


def dot_nt(a, b):
    return lax.dot_general(a, b, (((1,), (1,)), ((), ())), preferred_element_type=F32)


def pieces(x):
    high = x.astype(BF16).astype(F32)
    rest = x - high
    middle = rest.astype(BF16).astype(F32)
    return high, middle, (rest - middle).astype(BF16).astype(F32)


def span(offset, size):
    return min(offset, size - offset)


def farthest_first(first, second):
    offsets = [(a, b) for a in range(first) for b in range(second)]
    return sorted(offsets, key=lambda q: (-span(q[0], first) - span(q[1], second), q))


def ranks(side):
    return {offset: place for place, offset in enumerate(reversed(farthest_first(side, side)))}


class Place:
    def __init__(self, groups, regs, zn):
        self.groups, self.regs, self.zn = groups, regs, zn
        self.side = math.isqrt(regs // zn)
        self.grp = lax.axis_index("grp").astype(jnp.int32)
        reg = lax.axis_index("reg").astype(jnp.int32)
        self.z = lax.rem(reg, zn)
        self.yx = lax.div(reg, zn)
        self.y, self.x = lax.div(self.yx, self.side), lax.rem(self.yx, self.side)
        self.near = self.grp * zn + self.z
        self.rank = ranks(self.side)

    def shifted(self, core=0, y=0, x=0, z=0):
        c = lax.rem(self.grp + core, self.groups) if core else self.grp
        line = lax.rem(self.y + y, self.side) if y else self.y
        row = lax.rem(self.x + x, self.side) if x else self.x
        layer = self.z if isinstance(z, int) and z == 0 else lax.rem(self.z + z, self.zn)
        return c, line * self.side + row, layer

    def device(self, peer):
        return (peer[0], peer[1] * self.zn + peer[2])

    def opposite(self, y, x):
        return self.rank[(-y % self.side, -x % self.side)]

    def near_offsets(self):
        return [(c, z) for c, z in farthest_first(self.groups, self.zn) if (c, z) != (0, 0)]

    def far_offsets(self):
        return [(y, x) for y, x in farthest_first(self.side, self.side) if (y, x) != (0, 0)]


def send_part(source, target, rows, start, end, send, receive, device):
    part = pltpu.make_async_remote_copy(
        src_ref=source.at[pl.ds(start, rows)],
        dst_ref=target.at[pl.ds(end, rows)],
        send_sem=send,
        recv_sem=receive,
        device_id=device,
        device_id_type=MESH,
    )
    part.start()


def bytes_of(source, target, rows, send, receive, device):
    return pltpu.make_async_remote_copy(
        src_ref=source.at[pl.ds(0, rows)],
        dst_ref=target.at[pl.ds(0, rows)],
        send_sem=send,
        recv_sem=receive,
        device_id=device,
        device_id_type=MESH,
    )


def near_exchange(at, source, target, rows, send, receive):
    mine = pl.multiple_of(at.near * rows, rows)
    for core, z in at.near_offsets():
        peer = at.shifted(core=core, z=z)
        start = pl.multiple_of((peer[0] * at.zn + peer[2]) * rows, rows)
        send_part(source, target, rows, start, mine, send, receive, at.device(peer))
    target[pl.ds(mine, rows), :] = source[pl.ds(mine, rows), :]
    others = (at.groups * at.zn - 1) * rows
    return bytes_of(source, target, others, send, receive, at.device(at.shifted(core=1)))


def far_exchange(at, source, target, rows, send, receives):
    count = at.side * at.side
    for y, x in at.far_offsets():
        peer = at.shifted(y=y, x=x)
        start = pl.multiple_of(peer[1] * rows, rows)
        end = at.opposite(y, x)
        receive = receives.at[2 * end // count]
        send_part(source, target, rows, start, end * rows, send, receive, at.device(peer))
    target[0:rows, :] = source[pl.ds(pl.multiple_of(at.yx * rows, rows), rows), :]
    device = at.device(at.shifted(y=1))
    first, second = (count // 2 - 1) * rows, count // 2 * rows
    return (
        bytes_of(source, target, first, send, receives.at[0], device),
        bytes_of(source, target, second, send, receives.at[1], device),
    )


def direct(at, source, target, start_of, end_of, send, receive):
    zn = at.zn

    def ring(index):
        half = index // 2 if isinstance(index, int) else lax.div(index, 2)
        odd = index % 2 if isinstance(index, int) else lax.rem(index, 2)
        return zn // 2 + half - odd * (2 * half + 1)

    def layer(index, nearest):
        for y, x in farthest_first(at.side, at.side):
            for core in range(at.groups - 1, -1, -1):
                if nearest and y == x == core == 0:
                    continue
                peer = at.shifted(core=core, y=y, x=x, z=0 if nearest else ring(index))
                send_part(
                    source, target, 1, start_of(peer, y, x), end_of(y, x), send, receive,
                    at.device(peer),
                )

    def body(index, carry):
        layer(index, False)
        return carry

    lax.fori_loop(0, zn - 1, body, 0)
    layer(zn - 1, True)
    own = source[pl.ds(start_of(at.shifted(), 0, 0), 1), :]
    target[pl.ds(end_of(0, 0), 1), :] = own
    count = at.groups * at.regs - 1
    return bytes_of(source, target, count, send, receive, at.device(at.shifted(core=1)))


def turned(source, loose, target, major, minor):
    loose[...] = source[...].astype(F32)
    for index in range(minor):
        target[index * major : (index + 1) * major, :] = loose[
            pl.ds(index, major, stride=minor), :
        ].astype(BF16)


def picks(count, shape):
    row = lax.broadcasted_iota(jnp.int32, shape, 0)
    lane = lax.broadcasted_iota(jnp.int32, shape, 1)
    return jnp.where(count(row, lane), 1.0, 0.0).astype(BF16)


def staged(stages, count):
    for step in range(count + stages - 1):
        for stage in range(stages):
            if 0 <= step - stage < count:
                yield stage, step - stage


def kernel(
    sizes,
    *refs,
):
    arguments, results = refs[:10], refs[10:14]
    (
    send1, mid1, turn1, last1, loose, send2, last2, send3, last3, rows_s, words_s, words_b, onehot, freq_s, count_s, pick_s, phase0, phase1, depth_s, head_s,
    raw_s, graw_s, cot_b, w1t, w2t, w3t, w2, w3, wot, wo, encoded, hidden, slope, cotangents,
    acc1, acc2, acc3, acc4, colours, g_in, g_hid, g_head, sends, receives, local,
    ) = refs[24:]
    held = refs[14:24]
    anchors, directions, targets, regions, counts, depths, frequencies, w1, wh, w_head = held
    made = (colours, g_in, g_hid, g_head)
    groups, regs, zn, rays, segs, samples = sizes
    loads = [
        pltpu.make_async_copy(argument, place, local.at[index])
        for index, (argument, place) in enumerate(zip(arguments, held))
    ]
    n = groups * regs
    near, far = groups * zn, regs // zn
    slots = 2 * n
    width = segs * rays
    features = wh.shape[-1]
    freqs = features // 2

    at = Place(groups, regs, zn)

    def region_row(peer, y=0, x=0):
        return (peer[0] * zn + peer[2]) * far + peer[1]

    def source_row(peer, y, x):
        return at.rank[(y, x)] * near + peer[0] * zn + peer[2]

    barrier = pltpu.get_barrier_semaphore()
    greeted = [at.shifted(core=c, z=z) for c, z in at.near_offsets()]
    greeted += [at.shifted(y=y, x=x) for y, x in at.far_offsets()]
    for peer in greeted:
        pl.semaphore_signal(barrier, inc=1, device_id=at.device(peer), device_id_type=MESH)
    for load in loads:
        load.start()
    for index in (0, 1, 3, 4, 5):
        loads[index].wait()

    ids = regions[...]
    in_group = lax.rem(ids, regs)
    place = (lax.div(ids, regs) * zn + lax.rem(in_group, zn)) * far + lax.div(in_group, zn)
    rows_s[...] = jnp.full(rows_s.shape, -1, jnp.int32)
    words_s[...] = jnp.zeros(words_s.shape, F32)
    for k in range(segs):
        part = slice(k * rays, (k + 1) * rays)
        rows_s[0:1, part] = place[k : k + 1]
        both = jnp.concatenate([anchors[...], directions[...]], axis=0)
        high, middle, low = pieces(both)
        words_s[0:6, part] = high
        words_s[6:12, part] = middle
        words_s[12:18, part] = low
        words_s[18:19, part] = counts[k : k + 1].astype(F32)
        words_s[24 : 24 + samples, part] = depths[k].astype(F32)
    row_of = rows_s[0:1, :]
    match = row_of == lax.broadcasted_iota(jnp.int32, (n, width), 0)
    number = lax.broadcasted_iota(jnp.int32, (n, width), 1)
    last = jnp.max(jnp.where(match, number, -1), axis=1, keepdims=True)
    first_slot = number == last
    onehot[:, 0:width] = jnp.where(first_slot, 1.0, 0.0).astype(BF16)
    onehot[:, width:] = jnp.where(match & jnp.logical_not(first_slot), 1.0, 0.0).astype(BF16)
    words_b[...] = jnp.zeros(words_b.shape, BF16)
    packed = words_s[...].astype(BF16)
    words_b[0:32, 0:width] = packed
    words_b[32:64, width:] = packed
    send1[...] = dot_nt(onehot[...], words_b[...]).astype(BF16)

    pl.semaphore_wait(barrier, near + far - 2)

    near1 = near_exchange(at, send1, mid1, far, sends.at[0], receives.at[0])
    for index in (2, 6, 7, 8, 9):
        loads[index].wait()
    w1t[...] = (w1[0].astype(F32) * 0.5).T.astype(BF16)
    half2 = wh[0, 0].astype(F32) * 0.5
    w2[...] = half2.astype(BF16)
    w2t[...] = half2.T.astype(BF16)
    half3 = wh[0, 1].astype(F32) * 0.5
    w3[...] = half3.astype(BF16)
    w3t[...] = half3.T.astype(BF16)
    def first_words(row, lane):
        word, q, place = row & 15, row >> 4, lane - (row >> 4) * 32
        geometry = (word < 6) & ((place == word) | (place == word + 6) | (place == word + 12))
        single = ((word == 6) & (place == 18)) | ((word >= 8) & (place == word + 16))
        return (q < 2) & (place >= 0) & (place < 32) & (geometry | single)

    pick_s[0:32, :] = picks(first_words, (32, LANES))
    pick_s[32:64, :] = picks(lambda row, lane: row == lane, (32, LANES))
    pick_s[64:80, :] = picks(
        lambda row, lane: (row < 8) & (lane < 32) & (lane >> 4 == row >> 2)
        & (lane & 3 == row & 3) & (lane & 15 < 12),
        (16, LANES),
    )
    near1.wait_recv()
    turned(mid1, loose, turn1, near, far)
    halves = far_exchange(at, turn1, last1, near, sends.at[1], receives.at[pl.ds(1, 2)])
    head_s[...] = jnp.zeros(head_s.shape, F32)
    head_s[0:4, :] = w_head[...].astype(F32)
    wot[...] = head_s[...].astype(BF16)
    wo[...] = (head_s[...] * 0.5).T.astype(BF16)
    freq_s[...] = jnp.zeros(freq_s.shape, F32)
    freq_s[0:3, :] = frequencies[...] * (1.0 / (2.0 * math.pi))
    columns = freq_s[...].T
    send2[...] = jnp.zeros(send2.shape, F32)
    send3[...] = jnp.zeros(send3.shape, F32)
    graw_s[...] = jnp.zeros(graw_s.shape, F32)
    cot_b[...] = jnp.zeros(cot_b.shape, BF16)

    lane = n // 2
    part = 2 * lane

    def decode(half):
        words = dot_nt(pick_s[0:32, :], last1[half * lane : (half + 1) * lane, :])
        there = slice(half * part, (half + 1) * part)
        geometry = jnp.concatenate([words[0:8], words[16:24]], axis=1)
        count_s[:, there] = geometry
        base = jnp.zeros((freqs, part), F32)
        rate = jnp.zeros((freqs, part), F32)
        for c in range(3):
            base = base + columns[:, c : c + 1] * geometry[c : c + 1]
            rate = rate + columns[:, c : c + 1] * geometry[3 + c : 4 + c]
        phase0[:, there] = base
        phase1[:, there] = rate
        index = jnp.concatenate([words[8 : 8 + samples], words[24 : 24 + samples]], axis=1)
        depth_s[:, there] = 0.1 + (index + 0.5) * (2.0 / DEPTHS)

    layers = (w1t, w2t, w3t)
    for stage, item in staged(5, samples):
        half, first = divmod(2 * item, samples)
        there = slice(half * part, (half + 1) * part)
        if stage == 0:
            if first == 0:
                halves[half].wait_recv()
                decode(half)
            for side in range(2):
                turns = phase0[:, there] + depth_s[first + side : first + side + 1, there] * phase1[:, there]
                r = turns - jnp.round(turns)
                square = r * r
                sine = r * horner(SIN, square)
                columns_of = slice(side * part, (side + 1) * part)
                encoded[item, 0:freqs, columns_of] = (sine * horner(COS, square)).astype(BF16)
                encoded[item, freqs:, columns_of] = (1.0 - sine * sine).astype(BF16)
        elif stage < 4:
            z = dot(
                layers[stage - 1][...], encoded[item] if stage == 1 else hidden[stage - 2, item]
            )
            t = jnp.tanh(z)
            hidden[stage - 1, item] = (z + z * t).astype(BF16)
            slope[stage - 1, item] = t.astype(BF16)
        else:
            raw = dot(wot[...], hidden[2, item])
            for side in range(2):
                for k in range(4):
                    raw_s[k, first + side : first + side + 1, there] = raw[
                        k : k + 1, side * part : (side + 1) * part
                    ]

    live = jnp.where(
        lax.broadcasted_iota(jnp.int32, (samples, slots), 0).astype(F32) < count_s[6:7, :],
        1.0, 0.0,
    )
    density = raw_s[0]
    small = jnp.exp(-jnp.abs(density))
    softplus = jnp.maximum(density, 0.0) + jnp.log1p(small)
    clear = jnp.exp(-0.5 * softplus)
    alpha = live * (1.0 - clear)
    keep = 1.0 - alpha
    tone = [jax.nn.sigmoid(raw_s[1 + c]) for c in range(3)]
    through = jnp.ones((1, slots), F32)
    befores = []
    for i in range(samples):
        befores.append(through)
        through = through * keep[i : i + 1]
    before = jnp.concatenate(befores, axis=0)
    weight = before * alpha
    seg = [jnp.sum(weight * tone[c], axis=0, keepdims=True) for c in range(3)] + [through]
    answer = jnp.concatenate(seg, axis=0)
    blank = jnp.zeros((4, slots), F32)
    answer = jnp.concatenate(list(pieces(answer)) + [blank], axis=0)
    answer = jnp.concatenate(
        [
            jnp.concatenate([answer[:, 0:lane], answer[:, part : part + lane]], axis=1),
            jnp.concatenate([answer[:, lane:part], answer[:, part + lane :]], axis=1),
        ],
        axis=0,
    )
    send2[:, 0:32] = answer.T

    back = direct(
        at, send2, last2, source_row, lambda y, x: region_row(at.shifted()), sends.at[2],
        receives.at[3],
    )

    def slopes(item, carry):
        for index in range(3):
            h = hidden[index, item].astype(F32)
            t = slope[index, item].astype(F32)
            slope[index, item] = ((1.0 + h) + t * (1.0 - h)).astype(BF16)
        return carry

    lax.fori_loop(0, samples, slopes, 0)
    d_density = 0.5 * live * clear * jnp.where(density >= 0.0, 1.0, small) / (1.0 + small)
    d_tone = [weight * t * (1.0 - t) for t in tone]
    back.wait_recv()

    values = dot_nt(pick_s[32:64, :], last2[...].astype(BF16)).astype(BF16)
    found = dot(values[0:16], onehot[:, 0:width]) + dot(values[16:32], onehot[:, width:])
    found = (found[0:4] + found[4:8]) + found[8:12]
    arrive = [jnp.ones((1, rays), F32)]
    total = jnp.zeros((3, rays), F32)
    parts = []
    for k in range(segs):
        found_part = found[:, k * rays : (k + 1) * rays]
        parts.append(found_part)
        total = total + arrive[k] * found_part[0:3]
        arrive.append(arrive[k] * found_part[3:4])
    total = total + arrive[segs]
    colours[...] = total
    error = total - targets[...]
    behind = jnp.sum(error, axis=0, keepdims=True)
    for k in range(segs - 1, -1, -1):
        found_part = parts[k]
        cotangent = jnp.concatenate([arrive[k] * error, arrive[k] * behind], axis=0)
        behind = jnp.sum(error * found_part[0:3], axis=0, keepdims=True) + found_part[3:4] * behind
        stack = jnp.concatenate(
            list(pieces(cotangent)) + [jnp.zeros((4, rays), F32)], axis=0
        ).astype(BF16)
        cot_b[0:16, k * rays : (k + 1) * rays] = stack
        cot_b[16:32, width + k * rays : width + (k + 1) * rays] = stack
    send3[:, 0:32] = dot_nt(onehot[...], cot_b[...])

    forth = direct(
        at, send3, last3, region_row, lambda y, x: at.opposite(y, x) * near + at.near,
        sends.at[3], receives.at[4],
    )
    forth.wait_recv()

    words = dot_nt(pick_s[64:80, :], last3[...].astype(BF16))
    given = jnp.concatenate(
        [words[q : q + 4, there : there + lane] for there in (0, lane) for q in (0, 4)], axis=1
    )
    gain = given[0:1] * tone[0] + given[1:2] * tone[1] + given[2:3] * tone[2]
    after = given[3:4]
    backs = []
    for i in range(samples - 1, -1, -1):
        backs.append(befores[i] * (gain[i : i + 1] - after))
        after = alpha[i : i + 1] * gain[i : i + 1] + keep[i : i + 1] * after
    d_raw = [jnp.concatenate(backs[::-1], axis=0) * d_density]
    d_raw += [given[c : c + 1] * d_tone[c] for c in range(3)]
    for item in range(samples):
        half, first = divmod(2 * item, samples)
        for side in range(2):
            for k in range(4):
                graw_s[item, k : k + 1, side * part : (side + 1) * part] = d_raw[k][
                    first + side : first + side + 1, half * part : (half + 1) * part
                ]

    stores = [
        pltpu.make_async_copy(place, result, local.at[10 + index])
        for index, (place, result) in enumerate(zip(made, results))
    ]
    stores[0].start()
    backs = (wo, w3, w2)
    inputs = (lambda j: hidden[1, j], lambda j: hidden[0, j], lambda j: encoded[j])
    totals = (acc3, acc2, acc1)

    def gather(total, j, term):
        if j == 0:
            total[...] = term
        else:
            total[...] += term

    ends = (
        (3, g_head, lambda: acc4[0:4, :]),
        (2, g_hid.at[0, 1], lambda: acc3[...]),
        (2, g_hid.at[0, 0], lambda: acc2[...]),
        (1, g_in.at[0], lambda: acc1[...]),
    )
    for stage, j in staged(4, samples):
        if stage == 0:
            gather(acc4, j, dot_nt(graw_s[j].astype(BF16), hidden[2, j]))
        if stage < 3:
            g = graw_s[j].astype(BF16) if stage == 0 else cotangents[stage - 1, j]
            g = dot(backs[stage][...], g) * slope[2 - stage, j].astype(F32)
            cotangents[stage, j] = g.astype(BF16)
        if stage > 0:
            gather(totals[stage - 1], j, dot_nt(inputs[stage - 1](j), cotangents[stage - 1, j]))
        if j == samples - 1:
            index, place, value = ends[stage]
            place[...] = value().astype(BF16)
            if stage != 1:
                stores[index].start()

    for sent in (near1, *halves, back, forth):
        sent.wait_send()
    for store in stores:
        store.wait()


def hand_over(*refs):
    sources, results, places, sems = refs[:4], refs[4:8], refs[8:12], refs[12]
    loads = [
        pltpu.make_async_copy(sources[index], places[index], sems.at[index]) for index in range(4)
    ]
    stores = [
        pltpu.make_async_copy(places[index], results[index], sems.at[4 + index])
        for index in range(4)
    ]
    for load in loads:
        load.start()
    for load, store in zip(loads, stores):
        load.wait()
        store.start()
    for store in stores:
        store.wait()


def per_device(
    anchors, directions, targets, region_ids, sample_counts, depth_index, frequencies,
    w_input, w_hidden, w_head,
):
    groups, regs = lax.axis_size("grp"), lax.axis_size("reg")
    rays, segs = region_ids.shape
    samples = depth_index.shape[2]
    width = w_input.shape[1]
    zn = min(CHIPS_Z, regs)
    n = groups * regs
    slots = 2 * n
    near, far = groups * zn, regs // zn
    lanes = segs * rays
    board = [pltpu.VMEM((n, LANES), BF16)] * 4 + [pltpu.VMEM((n, LANES), F32)] * 5
    square = (width, width)
    operands = (
        anchors, directions, targets, region_ids.T, sample_counts.T,
        depth_index.transpose(1, 2, 0), frequencies, w_input, w_hidden, w_head[0].T,
    )
    shapes = (
        jax.ShapeDtypeStruct((3, rays), F32),
        jax.ShapeDtypeStruct(w_input.shape, BF16),
        jax.ShapeDtypeStruct(w_hidden.shape, BF16),
        jax.ShapeDtypeStruct((4, width), BF16),
    )
    scratch = [pltpu.VMEM(x.shape, x.dtype) for x in operands] + board + [
        pltpu.VMEM((8, lanes), jnp.int32),
        pltpu.VMEM((32, lanes), F32),
        pltpu.VMEM((LANES, 2 * lanes), BF16),
        pltpu.VMEM((n, 2 * lanes), BF16),
        pltpu.VMEM((8, width // 2), F32),
        pltpu.VMEM((8, slots), F32),
        pltpu.VMEM((80, LANES), BF16),
        pltpu.VMEM((width // 2, slots), F32),
        pltpu.VMEM((width // 2, slots), F32),
        pltpu.VMEM((samples, slots), F32),
        pltpu.VMEM((16, width), F32),
        pltpu.VMEM((4, samples, slots), F32),
        pltpu.VMEM((samples, 16, slots), F32),
        pltpu.VMEM((32, 2 * lanes), BF16),
        pltpu.VMEM(square, BF16),
        pltpu.VMEM(square, BF16),
        pltpu.VMEM(square, BF16),
        pltpu.VMEM(square, BF16),
        pltpu.VMEM(square, BF16),
        pltpu.VMEM((16, width), BF16),
        pltpu.VMEM((width, 16), BF16),
        pltpu.VMEM((samples, width, slots), BF16),
        pltpu.VMEM((3, samples, width, slots), BF16),
        pltpu.VMEM((3, samples, width, slots), BF16),
        pltpu.VMEM((3, samples, width, slots), BF16),
        pltpu.VMEM(square, F32),
        pltpu.VMEM(square, F32),
        pltpu.VMEM(square, F32),
        pltpu.VMEM((16, width), F32),
    ] + [pltpu.VMEM(x.shape, x.dtype) for x in shapes] + [
        pltpu.SemaphoreType.DMA((4,)),
        pltpu.SemaphoreType.DMA((5,)),
        pltpu.SemaphoreType.DMA((14,)),
    ]
    whole = pl.BlockSpec(memory_space=pltpu.HBM)
    made = pl.pallas_call(
        functools.partial(kernel, (groups, regs, zn, rays, segs, samples)),
        out_shape=shapes,
        in_specs=[whole] * 10,
        out_specs=[whole] * 4,
        scratch_shapes=scratch,
        compiler_params=pltpu.CompilerParams(
            collective_id=0, has_side_effects=True, vmem_limit_bytes=VMEM_BYTES
        ),
        name="radiance_step",
    )(*operands)
    colours, g_in, g_hid, g_head = pl.pallas_call(
        hand_over,
        out_shape=shapes,
        in_specs=[whole] * 4,
        out_specs=[whole] * 4,
        scratch_shapes=[pltpu.VMEM(x.shape, x.dtype) for x in shapes]
        + [pltpu.SemaphoreType.DMA((8,))],
        name="hand_over",
    )(*made)
    return colours, g_in, g_hid, g_head.T[None]


def solution(mesh):
    both = ("grp", "reg")
    return jax.shard_map(
        per_device,
        mesh=mesh,
        in_specs=(
            P(None, both), P(None, both), P(None, both), P(both, None), P(both, None),
            P(both, None, None), P(), P(both, None, None), P(both, None, None, None),
            P(both, None, None),
        ),
        out_specs=(
            P(None, both), P(both, None, None), P(both, None, None, None), P(both, None, None),
        ),
        check_vma=False,
    )
```

```python
import functools
import math

import jax
import jax.numpy as jnp
from jax import lax
from jax.experimental import pallas as pl
from jax.experimental.pallas import tpu as pltpu
from jax.sharding import PartitionSpec as P

DEPTHS = 128
CHIPS_Z = 8
VMEM_BYTES = 64 * 1024 * 1024
LANES = 128
MESH = pl.DeviceIdType.MESH
F32 = jnp.float32
BF16 = jnp.bfloat16

SIN = (4.442883014678955, -7.308241367340088, 3.6062893867492676, -0.8457654118537903,
       0.10920875519514084)
COS = (1.4142135381698608, -6.978850841522217, 5.7394609451293945, -1.8835630416870117,
       0.31069818139076233)


def horner(coefficients, x):
    total = jnp.full_like(x, coefficients[-1])
    for value in coefficients[-2::-1]:
        total = total * x + value
    return total


def dot(a, b):
    return jnp.dot(a, b, preferred_element_type=F32)


def dot_nt(a, b):
    return lax.dot_general(a, b, (((1,), (1,)), ((), ())), preferred_element_type=F32)


def pieces(x):
    high = x.astype(BF16).astype(F32)
    rest = x - high
    middle = rest.astype(BF16).astype(F32)
    return high, middle, (rest - middle).astype(BF16).astype(F32)


def span(offset, size):
    return min(offset, size - offset)


def farthest_first(first, second):
    offsets = [(a, b) for a in range(first) for b in range(second)]
    return sorted(offsets, key=lambda q: (-span(q[0], first) - span(q[1], second), q))


def ranks(side):
    return {offset: place for place, offset in enumerate(reversed(farthest_first(side, side)))}


class Place:
    def __init__(self, groups, regs, zn):
        self.groups, self.regs, self.zn = groups, regs, zn
        self.side = math.isqrt(regs // zn)
        self.grp = lax.axis_index("grp").astype(jnp.int32)
        reg = lax.axis_index("reg").astype(jnp.int32)
        self.z = lax.rem(reg, zn)
        self.yx = lax.div(reg, zn)
        self.y, self.x = lax.div(self.yx, self.side), lax.rem(self.yx, self.side)
        self.near = self.grp * zn + self.z
        self.rank = ranks(self.side)

        def turns(mine, size):
            return [mine] + [lax.rem(mine + step, size) for step in range(1, size)]

        self.cores = turns(self.grp, groups)
        self.layers = turns(self.z, zn)
        ys, xs = turns(self.y, self.side), turns(self.x, self.side)
        self.lines = {
            (y, x): ys[y] * self.side + xs[x] for y in range(self.side) for x in range(self.side)
        }

    def shifted(self, core=0, y=0, x=0, z=0):
        return self.cores[core], self.lines[(y, x)], self.layers[z]

    def device(self, peer):
        return (peer[0], peer[1] * self.zn + peer[2])

    def opposite(self, y, x):
        return self.rank[(-y % self.side, -x % self.side)]

    def near_offsets(self):
        return [(c, z) for c, z in farthest_first(self.groups, self.zn) if (c, z) != (0, 0)]

    def far_offsets(self):
        return [(y, x) for y, x in farthest_first(self.side, self.side) if (y, x) != (0, 0)]


def send_part(source, target, rows, start, end, send, receive, device):
    part = pltpu.make_async_remote_copy(
        src_ref=source.at[pl.ds(start, rows)],
        dst_ref=target.at[pl.ds(end, rows)],
        send_sem=send,
        recv_sem=receive,
        device_id=device,
        device_id_type=MESH,
    )
    part.start()


def bytes_of(source, target, rows, send, receive, device):
    return pltpu.make_async_remote_copy(
        src_ref=source.at[pl.ds(0, rows)],
        dst_ref=target.at[pl.ds(0, rows)],
        send_sem=send,
        recv_sem=receive,
        device_id=device,
        device_id_type=MESH,
    )


def near_exchange(at, source, target, rows, send, receive):
    mine = pl.multiple_of(at.near * rows, rows)
    for core, z in at.near_offsets():
        peer = at.shifted(core=core, z=z)
        start = pl.multiple_of((peer[0] * at.zn + peer[2]) * rows, rows)
        send_part(source, target, rows, start, mine, send, receive, at.device(peer))
    target[pl.ds(mine, rows), :] = source[pl.ds(mine, rows), :]
    others = (at.groups * at.zn - 1) * rows
    return bytes_of(source, target, others, send, receive, at.device(at.shifted(core=1)))


def far_exchange(at, source, target, rows, send, receives):
    count = at.side * at.side
    for y, x in at.far_offsets():
        peer = at.shifted(y=y, x=x)
        start = pl.multiple_of(peer[1] * rows, rows)
        end = at.opposite(y, x)
        receive = receives.at[2 * end // count]
        send_part(source, target, rows, start, end * rows, send, receive, at.device(peer))
    target[0:rows, :] = source[pl.ds(pl.multiple_of(at.yx * rows, rows), rows), :]
    device = at.device(at.shifted(y=1))
    first, second = (count // 2 - 1) * rows, count // 2 * rows
    return (
        bytes_of(source, target, first, send, receives.at[0], device),
        bytes_of(source, target, second, send, receives.at[1], device),
    )


def direct(at, source, target, start, end_of, send, receive):
    zn, side = at.zn, at.side
    lines = farthest_first(side, side)
    devices = {offset: at.lines[offset] * zn for offset in lines}
    starts = {offset: start[2](*offset) for offset in lines}
    ends = {offset: end_of(*offset) for offset in lines}
    bases = {
        (core, z): at.cores[core] * start[0] + at.layers[z] * start[1]
        for core in range(at.groups)
        for z in range(zn)
    }
    everyone = [(core, z, offset) for core, z in bases for offset in lines]

    def distance(peer):
        core, z, (y, x) = peer
        return core + span(z, zn) + span(y, side) + span(x, side)

    for core, z, offset in sorted(everyone, key=lambda peer: (-distance(peer), peer)):
        if distance((core, z, offset)):
            send_part(
                source, target, 1, bases[(core, z)] + starts[offset], ends[offset], send, receive,
                (at.cores[core], devices[offset] + at.layers[z]),
            )
    own = bases[(0, 0)] + starts[(0, 0)]
    target[pl.ds(ends[(0, 0)], 1), :] = source[pl.ds(own, 1), :]
    count = at.groups * at.regs - 1
    return bytes_of(source, target, count, send, receive, at.device(at.shifted(core=1)))


def turned(source, loose, target, major, minor):
    loose[...] = source[...].astype(F32)
    for index in range(minor):
        target[index * major : (index + 1) * major, :] = loose[
            pl.ds(index, major, stride=minor), :
        ].astype(BF16)


def staged(stages, count):
    for step in range(count + stages - 1):
        for stage in range(stages):
            if 0 <= step - stage < count:
                yield stage, step - stage


def kernel(
    sizes,
    *refs,
):
    arguments, results = refs[:10], refs[10:14]
    (
    send1, mid1, turn1, last1, loose, send2, last2, send3, last3, rows_s, words_s, words_b, onehot, freq_s, slots_s, phase0, phase1, depth_s, head_s,
    raw_s, graw_s, cot_b, w1t, w2t, w3t, w2, w3, wot, wo, encoded, hidden, slope, cotangents,
    acc1, acc2, acc3, acc4, colours, g_in, g_hid, g_head, sends, receives, local,
    ) = refs[24:]
    held = refs[14:24]
    anchors, directions, targets, regions, counts, depths, frequencies, w1, wh, w_head = held
    made = (colours, g_in, g_hid, g_head)
    groups, regs, zn, rays, segs, samples = sizes
    loads = [
        pltpu.make_async_copy(argument, place, local.at[index])
        for index, (argument, place) in enumerate(zip(arguments, held))
    ]
    for load in loads:
        load.start()
    n = groups * regs
    near, far = groups * zn, regs // zn
    slots = 2 * n
    width = segs * rays
    features = wh.shape[-1]
    freqs = features // 2

    at = Place(groups, regs, zn)

    region_row = (zn * far, far, lambda y, x: at.lines[(y, x)])
    source_row = (zn, 1, lambda y, x: at.rank[(y, x)] * near)
    my_region_row = at.near * far + at.yx
    barrier = pltpu.get_barrier_semaphore()
    greeted = [at.shifted(core=c, z=z) for c, z in at.near_offsets()]
    greeted += [at.shifted(y=y, x=x) for y, x in at.far_offsets()]
    for peer in greeted:
        pl.semaphore_signal(barrier, inc=1, device_id=at.device(peer), device_id_type=MESH)
    for index in (0, 1, 3, 4, 5):
        loads[index].wait()

    ids = regions[...]
    in_group = lax.rem(ids, regs)
    place = (lax.div(ids, regs) * zn + lax.rem(in_group, zn)) * far + lax.div(in_group, zn)
    rows_s[...] = jnp.full(rows_s.shape, -1, jnp.int32)
    words_s[...] = jnp.zeros(words_s.shape, F32)
    for k in range(segs):
        part = slice(k * rays, (k + 1) * rays)
        rows_s[0:1, part] = place[k : k + 1]
        both = jnp.concatenate([anchors[...], directions[...]], axis=0)
        high, middle, low = pieces(both)
        words_s[0:6, part] = high
        words_s[6:12, part] = middle
        words_s[12:18, part] = low
        words_s[18:19, part] = counts[k : k + 1].astype(F32)
        words_s[24 : 24 + samples, part] = depths[k].astype(F32)
    row_of = rows_s[0:1, :]
    match = row_of == lax.broadcasted_iota(jnp.int32, (n, width), 0)
    number = lax.broadcasted_iota(jnp.int32, (n, width), 1)
    last = jnp.max(jnp.where(match, number, -1), axis=1, keepdims=True)
    first_slot = number == last
    onehot[:, 0:width] = jnp.where(first_slot, 1.0, 0.0).astype(BF16)
    onehot[:, width:] = jnp.where(match & jnp.logical_not(first_slot), 1.0, 0.0).astype(BF16)
    words_b[...] = jnp.zeros(words_b.shape, BF16)
    packed = words_s[...].astype(BF16)
    words_b[0:32, 0:width] = packed
    words_b[32:64, width:] = packed
    send1[...] = dot_nt(onehot[...], words_b[...]).astype(BF16)

    pl.semaphore_wait(barrier, near + far - 2)

    near1 = near_exchange(at, send1, mid1, far, sends.at[0], receives.at[0])
    for index in (2, 6, 7, 8, 9):
        loads[index].wait()
    w1t[...] = (w1[0].astype(F32) * 0.5).T.astype(BF16)
    half2 = wh[0, 0].astype(F32) * 0.5
    w2[...] = half2.astype(BF16)
    w2t[...] = half2.T.astype(BF16)
    half3 = wh[0, 1].astype(F32) * 0.5
    w3[...] = half3.astype(BF16)
    w3t[...] = half3.T.astype(BF16)
    near1.wait_recv()
    turned(mid1, loose, turn1, near, far)
    halves = far_exchange(at, turn1, last1, near, sends.at[1], receives.at[pl.ds(1, 2)])
    head_s[...] = jnp.zeros(head_s.shape, F32)
    head_s[0:4, :] = w_head[...].astype(F32)
    wot[...] = head_s[...].astype(BF16)
    wo[...] = (head_s[...] * 0.5).T.astype(BF16)
    freq_s[...] = jnp.zeros(freq_s.shape, F32)
    freq_s[0:3, :] = frequencies[...] * (1.0 / (2.0 * math.pi))
    columns = freq_s[...].T
    send2[...] = jnp.zeros(send2.shape, F32)
    send3[...] = jnp.zeros(send3.shape, F32)
    graw_s[...] = jnp.zeros(graw_s.shape, F32)
    cot_b[...] = jnp.zeros(cot_b.shape, BF16)

    lane = n // 2
    part = 2 * lane

    def decode(half):
        words = last1[half * lane : (half + 1) * lane, :].astype(F32).T
        there = slice(half * part, (half + 1) * part)
        slots_s[:, half * part : half * part + lane] = words[0:32]
        slots_s[:, half * part + lane : (half + 1) * part] = words[32:64]
        geometry = (slots_s[0:6, there] + slots_s[6:12, there]) + slots_s[12:18, there]
        base = jnp.zeros((freqs, part), F32)
        rate = jnp.zeros((freqs, part), F32)
        for c in range(3):
            base = base + columns[:, c : c + 1] * geometry[c : c + 1]
            rate = rate + columns[:, c : c + 1] * geometry[3 + c : 4 + c]
        phase0[:, there] = base
        phase1[:, there] = rate
        depth_s[:, there] = 0.1 + (slots_s[24 : 24 + samples, there] + 0.5) * (2.0 / DEPTHS)

    layers = (w1t, w2t, w3t)
    for stage, item in staged(5, samples):
        half, first = divmod(2 * item, samples)
        there = slice(half * part, (half + 1) * part)
        if stage == 0:
            if first == 0:
                halves[half].wait_recv()
                decode(half)
            for side in range(2):
                turns = phase0[:, there] + depth_s[first + side : first + side + 1, there] * phase1[:, there]
                r = turns - jnp.round(turns)
                square = r * r
                sine = r * horner(SIN, square)
                columns_of = slice(side * part, (side + 1) * part)
                encoded[item, 0:freqs, columns_of] = (sine * horner(COS, square)).astype(BF16)
                encoded[item, freqs:, columns_of] = (1.0 - sine * sine).astype(BF16)
        elif stage < 4:
            z = dot(
                layers[stage - 1][...], encoded[item] if stage == 1 else hidden[stage - 2, item]
            )
            t = jnp.tanh(z)
            hidden[stage - 1, item] = (z + z * t).astype(BF16)
            slope[stage - 1, item] = t.astype(BF16)
        else:
            raw = dot(wot[...], hidden[2, item])
            for side in range(2):
                for k in range(4):
                    raw_s[k, first + side : first + side + 1, there] = raw[
                        k : k + 1, side * part : (side + 1) * part
                    ]

    live = jnp.where(
        lax.broadcasted_iota(jnp.int32, (samples, slots), 0).astype(F32) < slots_s[18:19, :],
        1.0, 0.0,
    )
    density = raw_s[0]
    small = jnp.exp(-jnp.abs(density))
    softplus = jnp.maximum(density, 0.0) + jnp.log1p(small)
    clear = jnp.exp(-0.5 * softplus)
    alpha = live * (1.0 - clear)
    keep = 1.0 - alpha
    tone = [jax.nn.sigmoid(raw_s[1 + c]) for c in range(3)]
    through = jnp.ones((1, slots), F32)
    befores = []
    for i in range(samples):
        befores.append(through)
        through = through * keep[i : i + 1]
    before = jnp.concatenate(befores, axis=0)
    weight = before * alpha
    seg = [jnp.sum(weight * tone[c], axis=0, keepdims=True) for c in range(3)] + [through]
    answer = jnp.concatenate(seg, axis=0)
    blank = jnp.zeros((4, slots), F32)
    answer = jnp.concatenate(list(pieces(answer)) + [blank], axis=0)
    answer = jnp.concatenate(
        [
            jnp.concatenate([answer[:, 0:lane], answer[:, part : part + lane]], axis=1),
            jnp.concatenate([answer[:, lane:part], answer[:, part + lane :]], axis=1),
        ],
        axis=0,
    )
    send2[:, 0:32] = answer.T

    back = direct(
        at, send2, last2, source_row, lambda y, x: my_region_row, sends.at[2], receives.at[3]
    )

    def slopes(item, carry):
        for index in range(3):
            h = hidden[index, item].astype(F32)
            t = slope[index, item].astype(F32)
            slope[index, item] = ((1.0 + h) + t * (1.0 - h)).astype(BF16)
        return carry

    lax.fori_loop(0, samples, slopes, 0)
    d_density = 0.5 * live * clear * jnp.where(density >= 0.0, 1.0, small) / (1.0 + small)
    d_tone = [weight * t * (1.0 - t) for t in tone]
    back.wait_recv()

    values = last2[...].T[0:32].astype(BF16)
    found = dot(values[0:16], onehot[:, 0:width]) + dot(values[16:32], onehot[:, width:])
    found = (found[0:4] + found[4:8]) + found[8:12]
    arrive = [jnp.ones((1, rays), F32)]
    total = jnp.zeros((3, rays), F32)
    parts = []
    for k in range(segs):
        found_part = found[:, k * rays : (k + 1) * rays]
        parts.append(found_part)
        total = total + arrive[k] * found_part[0:3]
        arrive.append(arrive[k] * found_part[3:4])
    total = total + arrive[segs]
    colours[...] = total
    error = total - targets[...]
    behind = jnp.sum(error, axis=0, keepdims=True)
    for k in range(segs - 1, -1, -1):
        found_part = parts[k]
        cotangent = jnp.concatenate([arrive[k] * error, arrive[k] * behind], axis=0)
        behind = jnp.sum(error * found_part[0:3], axis=0, keepdims=True) + found_part[3:4] * behind
        stack = jnp.concatenate(
            list(pieces(cotangent)) + [jnp.zeros((4, rays), F32)], axis=0
        ).astype(BF16)
        cot_b[0:16, k * rays : (k + 1) * rays] = stack
        cot_b[16:32, width + k * rays : width + (k + 1) * rays] = stack
    send3[:, 0:32] = dot_nt(onehot[...], cot_b[...])

    forth = direct(
        at, send3, last3, region_row, lambda y, x: at.opposite(y, x) * near + at.near,
        sends.at[3], receives.at[4],
    )
    forth.wait_recv()

    words = last3[...].T[0:32]
    given = [
        (words[q : q + 4] + words[q + 4 : q + 8]) + words[q + 8 : q + 12] for q in (0, 16)
    ]
    given = jnp.concatenate(
        [given[0][:, 0:lane], given[1][:, 0:lane], given[0][:, lane:], given[1][:, lane:]], axis=1
    )
    gain = given[0:1] * tone[0] + given[1:2] * tone[1] + given[2:3] * tone[2]
    after = given[3:4]
    backs = []
    for i in range(samples - 1, -1, -1):
        backs.append(befores[i] * (gain[i : i + 1] - after))
        after = alpha[i : i + 1] * gain[i : i + 1] + keep[i : i + 1] * after
    d_raw = [jnp.concatenate(backs[::-1], axis=0) * d_density]
    d_raw += [given[c : c + 1] * d_tone[c] for c in range(3)]
    for item in range(samples):
        half, first = divmod(2 * item, samples)
        for side in range(2):
            for k in range(4):
                graw_s[item, k : k + 1, side * part : (side + 1) * part] = d_raw[k][
                    first + side : first + side + 1, half * part : (half + 1) * part
                ]

    stores = [
        pltpu.make_async_copy(place, result, local.at[10 + index])
        for index, (place, result) in enumerate(zip(made, results))
    ]
    stores[0].start()
    backs = (wo, w3, w2)
    inputs = (lambda j: hidden[1, j], lambda j: hidden[0, j], lambda j: encoded[j])
    totals = (acc3, acc2, acc1)

    def gather(total, j, term):
        if j == 0:
            total[...] = term
        else:
            total[...] += term

    ends = (
        (3, g_head, lambda: acc4[0:4, :]),
        (2, g_hid.at[0, 1], lambda: acc3[...]),
        (2, g_hid.at[0, 0], lambda: acc2[...]),
        (1, g_in.at[0], lambda: acc1[...]),
    )
    for stage, j in staged(4, samples):
        if stage == 0:
            gather(acc4, j, dot_nt(graw_s[j].astype(BF16), hidden[2, j]))
        if stage < 3:
            g = graw_s[j].astype(BF16) if stage == 0 else cotangents[stage - 1, j]
            g = dot(backs[stage][...], g) * slope[2 - stage, j].astype(F32)
            cotangents[stage, j] = g.astype(BF16)
        if stage > 0:
            gather(totals[stage - 1], j, dot_nt(inputs[stage - 1](j), cotangents[stage - 1, j]))
        if j == samples - 1:
            index, place, value = ends[stage]
            place[...] = value().astype(BF16)
            if stage != 1:
                stores[index].start()

    for sent in (near1, *halves, back, forth):
        sent.wait_send()
    for store in stores:
        store.wait()


def hand_over(*refs):
    sources, results, places, sems = refs[:4], refs[4:8], refs[8:12], refs[12]
    width = sources[1].shape[1]
    half = width // 2
    pieces_of = [(0, ()), (3, ())]
    pieces_of += [(2, (0, k, pl.ds(h, half))) for k in range(2) for h in (0, half)]
    pieces_of += [(1, (0, pl.ds(h, half))) for h in (0, half)]

    def part(group, index, where):
        return group[index].at[where] if where else group[index]

    moves = [
        tuple(
            pltpu.make_async_copy(part(a, index, where), part(b, index, where), sems.at[row, number])
            for row, (a, b) in enumerate(((sources, places), (places, results)))
        )
        for number, (index, where) in enumerate(pieces_of)
    ]
    for load, _ in moves:
        load.start()
    for load, store in moves:
        load.wait()
        store.start()
    for _, store in moves:
        store.wait()


def per_device(
    anchors, directions, targets, region_ids, sample_counts, depth_index, frequencies,
    w_input, w_hidden, w_head,
):
    groups, regs = lax.axis_size("grp"), lax.axis_size("reg")
    rays, segs = region_ids.shape
    samples = depth_index.shape[2]
    width = w_input.shape[1]
    zn = min(CHIPS_Z, regs)
    n = groups * regs
    slots = 2 * n
    near, far = groups * zn, regs // zn
    lanes = segs * rays
    board = [pltpu.VMEM((n, LANES), BF16)] * 4 + [pltpu.VMEM((n, LANES), F32)] * 5
    square = (width, width)
    operands = (
        anchors, directions, targets, region_ids.T, sample_counts.T,
        depth_index.transpose(1, 2, 0), frequencies, w_input, w_hidden, w_head[0].T,
    )
    shapes = (
        jax.ShapeDtypeStruct((3, rays), F32),
        jax.ShapeDtypeStruct(w_input.shape, BF16),
        jax.ShapeDtypeStruct(w_hidden.shape, BF16),
        jax.ShapeDtypeStruct((4, width), BF16),
    )
    scratch = [pltpu.VMEM(x.shape, x.dtype) for x in operands] + board + [
        pltpu.VMEM((8, lanes), jnp.int32),
        pltpu.VMEM((32, lanes), F32),
        pltpu.VMEM((LANES, 2 * lanes), BF16),
        pltpu.VMEM((n, 2 * lanes), BF16),
        pltpu.VMEM((8, width // 2), F32),
        pltpu.VMEM((32, slots), F32),
        pltpu.VMEM((width // 2, slots), F32),
        pltpu.VMEM((width // 2, slots), F32),
        pltpu.VMEM((samples, slots), F32),
        pltpu.VMEM((16, width), F32),
        pltpu.VMEM((4, samples, slots), F32),
        pltpu.VMEM((samples, 16, slots), F32),
        pltpu.VMEM((32, 2 * lanes), BF16),
        pltpu.VMEM(square, BF16),
        pltpu.VMEM(square, BF16),
        pltpu.VMEM(square, BF16),
        pltpu.VMEM(square, BF16),
        pltpu.VMEM(square, BF16),
        pltpu.VMEM((16, width), BF16),
        pltpu.VMEM((width, 16), BF16),
        pltpu.VMEM((samples, width, slots), BF16),
        pltpu.VMEM((3, samples, width, slots), BF16),
        pltpu.VMEM((3, samples, width, slots), BF16),
        pltpu.VMEM((3, samples, width, slots), BF16),
        pltpu.VMEM(square, F32),
        pltpu.VMEM(square, F32),
        pltpu.VMEM(square, F32),
        pltpu.VMEM((16, width), F32),
    ] + [pltpu.VMEM(x.shape, x.dtype) for x in shapes] + [
        pltpu.SemaphoreType.DMA((4,)),
        pltpu.SemaphoreType.DMA((5,)),
        pltpu.SemaphoreType.DMA((14,)),
    ]
    whole = pl.BlockSpec(memory_space=pltpu.HBM)
    made = pl.pallas_call(
        functools.partial(kernel, (groups, regs, zn, rays, segs, samples)),
        out_shape=shapes,
        in_specs=[whole] * 10,
        out_specs=[whole] * 4,
        scratch_shapes=scratch,
        compiler_params=pltpu.CompilerParams(
            collective_id=0, has_side_effects=True, vmem_limit_bytes=VMEM_BYTES
        ),
        name="radiance_step",
    )(*operands)
    colours, g_in, g_hid, g_head = pl.pallas_call(
        hand_over,
        out_shape=shapes,
        in_specs=[whole] * 4,
        out_specs=[whole] * 4,
        scratch_shapes=[pltpu.VMEM(x.shape, x.dtype) for x in shapes]
        + [pltpu.SemaphoreType.DMA((2, 8))],
        name="hand_over",
    )(*made)
    return colours, g_in, g_hid, g_head.T[None]


def solution(mesh):
    both = ("grp", "reg")
    return jax.shard_map(
        per_device,
        mesh=mesh,
        in_specs=(
            P(None, both), P(None, both), P(None, both), P(both, None), P(both, None),
            P(both, None, None), P(), P(both, None, None), P(both, None, None, None),
            P(both, None, None),
        ),
        out_specs=(
            P(None, both), P(both, None, None), P(both, None, None, None), P(both, None, None),
        ),
        check_vma=False,
    )
```

```python
import functools
import math

import jax
import jax.numpy as jnp
from jax import lax
from jax.experimental import pallas as pl
from jax.experimental.pallas import tpu as pltpu
from jax.sharding import PartitionSpec as P

DEPTHS = 128
CHIPS_Z = 8
VMEM_BYTES = 64 * 1024 * 1024
LANES = 128
MESH = pl.DeviceIdType.MESH
F32 = jnp.float32
BF16 = jnp.bfloat16

SIN = (4.442883014678955, -7.308241367340088, 3.6062893867492676, -0.8457654118537903,
       0.10920875519514084)
COS = (1.4142135381698608, -6.978850841522217, 5.7394609451293945, -1.8835630416870117,
       0.31069818139076233)


def horner(coefficients, x):
    total = jnp.full_like(x, coefficients[-1])
    for value in coefficients[-2::-1]:
        total = total * x + value
    return total


def dot(a, b):
    return jnp.dot(a, b, preferred_element_type=F32)


def dot_nt(a, b):
    return lax.dot_general(a, b, (((1,), (1,)), ((), ())), preferred_element_type=F32)


def pieces(x):
    high = x.astype(BF16).astype(F32)
    rest = x - high
    middle = rest.astype(BF16).astype(F32)
    return high, middle, (rest - middle).astype(BF16).astype(F32)


def span(offset, size):
    return min(offset, size - offset)


def farthest_first(first, second):
    offsets = [(a, b) for a in range(first) for b in range(second)]
    return sorted(offsets, key=lambda q: (-span(q[0], first) - span(q[1], second), q))


def ranks(side):
    return {offset: place for place, offset in enumerate(reversed(farthest_first(side, side)))}


class Place:
    def __init__(self, groups, regs, zn):
        self.groups, self.regs, self.zn = groups, regs, zn
        self.side = math.isqrt(regs // zn)
        self.grp = lax.axis_index("grp").astype(jnp.int32)
        reg = lax.axis_index("reg").astype(jnp.int32)
        self.z = lax.rem(reg, zn)
        self.yx = lax.div(reg, zn)
        self.y, self.x = lax.div(self.yx, self.side), lax.rem(self.yx, self.side)
        self.near = self.grp * zn + self.z
        self.rank = ranks(self.side)

        def turns(mine, size):
            return [mine] + [lax.rem(mine + step, size) for step in range(1, size)]

        self.cores = turns(self.grp, groups)
        self.layers = turns(self.z, zn)
        ys, xs = turns(self.y, self.side), turns(self.x, self.side)
        self.lines = {
            (y, x): ys[y] * self.side + xs[x] for y in range(self.side) for x in range(self.side)
        }

    def shifted(self, core=0, y=0, x=0, z=0):
        return self.cores[core], self.lines[(y, x)], self.layers[z]

    def device(self, peer):
        return (peer[0], peer[1] * self.zn + peer[2])

    def opposite(self, y, x):
        return self.rank[(-y % self.side, -x % self.side)]

    def near_offsets(self):
        return [(c, z) for c, z in farthest_first(self.groups, self.zn) if (c, z) != (0, 0)]

    def far_offsets(self):
        return [(y, x) for y, x in farthest_first(self.side, self.side) if (y, x) != (0, 0)]


def send_part(source, target, rows, start, end, send, receive, device):
    part = pltpu.make_async_remote_copy(
        src_ref=source.at[pl.ds(start, rows)],
        dst_ref=target.at[pl.ds(end, rows)],
        send_sem=send,
        recv_sem=receive,
        device_id=device,
        device_id_type=MESH,
    )
    part.start()


def bytes_of(source, target, rows, send, receive, device):
    return pltpu.make_async_remote_copy(
        src_ref=source.at[pl.ds(0, rows)],
        dst_ref=target.at[pl.ds(0, rows)],
        send_sem=send,
        recv_sem=receive,
        device_id=device,
        device_id_type=MESH,
    )


def near_exchange(at, source, target, rows, send, receive):
    mine = pl.multiple_of(at.near * rows, rows)
    for core, z in at.near_offsets():
        peer = at.shifted(core=core, z=z)
        start = pl.multiple_of((peer[0] * at.zn + peer[2]) * rows, rows)
        send_part(source, target, rows, start, mine, send, receive, at.device(peer))
    target[pl.ds(mine, rows), :] = source[pl.ds(mine, rows), :]
    others = (at.groups * at.zn - 1) * rows
    return bytes_of(source, target, others, send, receive, at.device(at.shifted(core=1)))


def far_exchange(at, source, target, rows, send, receives):
    count = at.side * at.side
    for y, x in at.far_offsets():
        peer = at.shifted(y=y, x=x)
        start = pl.multiple_of(peer[1] * rows, rows)
        end = at.opposite(y, x)
        receive = receives.at[2 * end // count]
        send_part(source, target, rows, start, end * rows, send, receive, at.device(peer))
    target[0:rows, :] = source[pl.ds(pl.multiple_of(at.yx * rows, rows), rows), :]
    device = at.device(at.shifted(y=1))
    first, second = (count // 2 - 1) * rows, count // 2 * rows
    return (
        bytes_of(source, target, first, send, receives.at[0], device),
        bytes_of(source, target, second, send, receives.at[1], device),
    )


def direct(at, source, target, start, end_of, send, receive):
    zn, side = at.zn, at.side
    lines = farthest_first(side, side)
    devices = {offset: at.lines[offset] * zn for offset in lines}
    starts = {offset: start[2](*offset) for offset in lines}
    ends = {offset: end_of(*offset) for offset in lines}
    bases = {
        (core, z): at.cores[core] * start[0] + at.layers[z] * start[1]
        for core in range(at.groups)
        for z in range(zn)
    }
    everyone = [(core, z, offset) for core, z in bases for offset in lines]

    def distance(peer):
        core, z, (y, x) = peer
        return core + span(z, zn) + span(y, side) + span(x, side)

    for core, z, offset in sorted(everyone, key=lambda peer: (-distance(peer), peer)):
        if distance((core, z, offset)):
            send_part(
                source, target, 1, bases[(core, z)] + starts[offset], ends[offset], send, receive,
                (at.cores[core], devices[offset] + at.layers[z]),
            )
    own = bases[(0, 0)] + starts[(0, 0)]
    target[pl.ds(ends[(0, 0)], 1), :] = source[pl.ds(own, 1), :]
    count = at.groups * at.regs - 1
    return bytes_of(source, target, count, send, receive, at.device(at.shifted(core=1)))


def turned(source, loose, target, major, minor):
    loose[...] = source[...].astype(F32)
    for index in range(minor):
        target[index * major : (index + 1) * major, :] = loose[
            pl.ds(index, major, stride=minor), :
        ].astype(BF16)


def staged(stages, count):
    for step in range(count + stages - 1):
        for stage in range(stages):
            if 0 <= step - stage < count:
                yield stage, step - stage


def kernel(
    sizes,
    *refs,
):
    arguments, results = refs[:10], refs[10:14]
    (
    send1, mid1, turn1, last1, loose, send2, last2, send3, last3, rows_s, words_s, words_b, onehot, freq_s, slots_s, phase0, phase1, depth_s, head_s,
    raw_s, graw_s, cot_b, w1t, w2t, w3t, w2, w3, wot, wo, encoded, hidden, slope, cotangents,
    acc1, acc2, acc3, acc4, colours, g_in, g_hid, g_head, sends, receives, local,
    ) = refs[24:]
    held = refs[14:24]
    anchors, directions, targets, regions, counts, depths, frequencies, w1, wh, w_head = held
    made = (colours, g_in, g_hid, g_head)
    groups, regs, zn, rays, segs, samples = sizes
    loads = [
        pltpu.make_async_copy(argument, place, local.at[index])
        for index, (argument, place) in enumerate(zip(arguments, held))
    ]
    n = groups * regs
    near, far = groups * zn, regs // zn
    slots = 2 * n
    width = segs * rays
    features = wh.shape[-1]
    freqs = features // 2

    at = Place(groups, regs, zn)

    region_row = (zn * far, far, lambda y, x: at.lines[(y, x)])
    source_row = (zn, 1, lambda y, x: at.rank[(y, x)] * near)
    my_region_row = at.near * far + at.yx
    barrier = pltpu.get_barrier_semaphore()
    greeted = [at.shifted(core=c, z=z) for c, z in at.near_offsets()]
    greeted += [at.shifted(y=y, x=x) for y, x in at.far_offsets()]
    for peer in greeted:
        pl.semaphore_signal(barrier, inc=1, device_id=at.device(peer), device_id_type=MESH)
    for load in loads:
        load.start()
    for index in (0, 1, 3, 4, 5):
        loads[index].wait()

    ids = regions[...]
    in_group = lax.rem(ids, regs)
    place = (lax.div(ids, regs) * zn + lax.rem(in_group, zn)) * far + lax.div(in_group, zn)
    rows_s[...] = jnp.full(rows_s.shape, -1, jnp.int32)
    words_s[...] = jnp.zeros(words_s.shape, F32)
    for k in range(segs):
        part = slice(k * rays, (k + 1) * rays)
        rows_s[0:1, part] = place[k : k + 1]
        both = jnp.concatenate([anchors[...], directions[...]], axis=0)
        high, middle, low = pieces(both)
        words_s[0:6, part] = high
        words_s[6:12, part] = middle
        words_s[12:18, part] = low
        words_s[18:19, part] = counts[k : k + 1].astype(F32)
        words_s[24 : 24 + samples, part] = depths[k].astype(F32)
    row_of = rows_s[0:1, :]
    match = row_of == lax.broadcasted_iota(jnp.int32, (n, width), 0)
    number = lax.broadcasted_iota(jnp.int32, (n, width), 1)
    last = jnp.max(jnp.where(match, number, -1), axis=1, keepdims=True)
    first_slot = number == last
    onehot[:, 0:width] = jnp.where(first_slot, 1.0, 0.0).astype(BF16)
    onehot[:, width:] = jnp.where(match & jnp.logical_not(first_slot), 1.0, 0.0).astype(BF16)
    words_b[...] = jnp.zeros(words_b.shape, BF16)
    packed = words_s[...].astype(BF16)
    words_b[0:32, 0:width] = packed
    words_b[32:64, width:] = packed
    send1[...] = dot_nt(onehot[...], words_b[...]).astype(BF16)

    pl.semaphore_wait(barrier, near + far - 2)

    near1 = near_exchange(at, send1, mid1, far, sends.at[0], receives.at[0])
    for index in (2, 6, 7, 8, 9):
        loads[index].wait()
    w1t[...] = (w1[0].astype(F32) * 0.5).T.astype(BF16)
    half2 = wh[0, 0].astype(F32) * 0.5
    w2[...] = half2.astype(BF16)
    w2t[...] = half2.T.astype(BF16)
    half3 = wh[0, 1].astype(F32) * 0.5
    w3[...] = half3.astype(BF16)
    w3t[...] = half3.T.astype(BF16)
    near1.wait_recv()
    turned(mid1, loose, turn1, near, far)
    halves = far_exchange(at, turn1, last1, near, sends.at[1], receives.at[pl.ds(1, 2)])
    head_s[...] = jnp.zeros(head_s.shape, F32)
    head_s[0:4, :] = w_head[...].astype(F32)
    wot[...] = head_s[...].astype(BF16)
    wo[...] = (head_s[...] * 0.5).T.astype(BF16)
    freq_s[...] = jnp.zeros(freq_s.shape, F32)
    freq_s[0:3, :] = frequencies[...] * (1.0 / (2.0 * math.pi))
    columns = freq_s[...].T
    send2[...] = jnp.zeros(send2.shape, F32)
    send3[...] = jnp.zeros(send3.shape, F32)
    graw_s[...] = jnp.zeros(graw_s.shape, F32)
    cot_b[...] = jnp.zeros(cot_b.shape, BF16)

    lane = n // 2
    part = 2 * lane

    def decode(half):
        words = last1[half * lane : (half + 1) * lane, :].astype(F32).T
        there = slice(half * part, (half + 1) * part)
        slots_s[:, half * part : half * part + lane] = words[0:32]
        slots_s[:, half * part + lane : (half + 1) * part] = words[32:64]
        geometry = (slots_s[0:6, there] + slots_s[6:12, there]) + slots_s[12:18, there]
        base = jnp.zeros((freqs, part), F32)
        rate = jnp.zeros((freqs, part), F32)
        for c in range(3):
            base = base + columns[:, c : c + 1] * geometry[c : c + 1]
            rate = rate + columns[:, c : c + 1] * geometry[3 + c : 4 + c]
        phase0[:, there] = base
        phase1[:, there] = rate
        depth_s[:, there] = 0.1 + (slots_s[24 : 24 + samples, there] + 0.5) * (2.0 / DEPTHS)

    layers = (w1t, w2t, w3t)
    for stage, item in staged(5, samples):
        half, first = divmod(2 * item, samples)
        there = slice(half * part, (half + 1) * part)
        if stage == 0:
            if first == 0:
                halves[half].wait_recv()
                decode(half)
            for side in range(2):
                turns = phase0[:, there] + depth_s[first + side : first + side + 1, there] * phase1[:, there]
                r = turns - jnp.round(turns)
                square = r * r
                sine = r * horner(SIN, square)
                columns_of = slice(side * part, (side + 1) * part)
                encoded[item, 0:freqs, columns_of] = (sine * horner(COS, square)).astype(BF16)
                encoded[item, freqs:, columns_of] = (1.0 - sine * sine).astype(BF16)
        elif stage < 4:
            z = dot(
                layers[stage - 1][...], encoded[item] if stage == 1 else hidden[stage - 2, item]
            )
            t = jnp.tanh(z)
            hidden[stage - 1, item] = (z + z * t).astype(BF16)
            slope[stage - 1, item] = t.astype(BF16)
        else:
            raw = dot(wot[...], hidden[2, item])
            for side in range(2):
                for k in range(4):
                    raw_s[k, first + side : first + side + 1, there] = raw[
                        k : k + 1, side * part : (side + 1) * part
                    ]

    live = jnp.where(
        lax.broadcasted_iota(jnp.int32, (samples, slots), 0).astype(F32) < slots_s[18:19, :],
        1.0, 0.0,
    )
    density = raw_s[0]
    small = jnp.exp(-jnp.abs(density))
    softplus = jnp.maximum(density, 0.0) + jnp.log1p(small)
    clear = jnp.exp(-0.5 * softplus)
    alpha = live * (1.0 - clear)
    keep = 1.0 - alpha
    tone = [jax.nn.sigmoid(raw_s[1 + c]) for c in range(3)]
    through = jnp.ones((1, slots), F32)
    befores = []
    for i in range(samples):
        befores.append(through)
        through = through * keep[i : i + 1]
    before = jnp.concatenate(befores, axis=0)
    weight = before * alpha
    seg = [jnp.sum(weight * tone[c], axis=0, keepdims=True) for c in range(3)] + [through]
    answer = jnp.concatenate(seg, axis=0)
    blank = jnp.zeros((4, slots), F32)
    answer = jnp.concatenate(list(pieces(answer)) + [blank], axis=0)
    answer = jnp.concatenate(
        [
            jnp.concatenate([answer[:, 0:lane], answer[:, part : part + lane]], axis=1),
            jnp.concatenate([answer[:, lane:part], answer[:, part + lane :]], axis=1),
        ],
        axis=0,
    )
    send2[:, 0:32] = answer.T

    back = direct(
        at, send2, last2, source_row, lambda y, x: my_region_row, sends.at[2], receives.at[3]
    )

    def slopes(item, carry):
        for index in range(3):
            h = hidden[index, item].astype(F32)
            t = slope[index, item].astype(F32)
            slope[index, item] = ((1.0 + h) + t * (1.0 - h)).astype(BF16)
        return carry

    lax.fori_loop(0, samples, slopes, 0)
    d_density = 0.5 * live * clear * jnp.where(density >= 0.0, 1.0, small) / (1.0 + small)
    d_tone = [weight * t * (1.0 - t) for t in tone]
    back.wait_recv()

    values = last2[...].T[0:32].astype(BF16)
    found = dot(values[0:16], onehot[:, 0:width]) + dot(values[16:32], onehot[:, width:])
    found = (found[0:4] + found[4:8]) + found[8:12]
    arrive = [jnp.ones((1, rays), F32)]
    total = jnp.zeros((3, rays), F32)
    parts = []
    for k in range(segs):
        found_part = found[:, k * rays : (k + 1) * rays]
        parts.append(found_part)
        total = total + arrive[k] * found_part[0:3]
        arrive.append(arrive[k] * found_part[3:4])
    total = total + arrive[segs]
    colours[...] = total
    error = total - targets[...]
    behind = jnp.sum(error, axis=0, keepdims=True)
    for k in range(segs - 1, -1, -1):
        found_part = parts[k]
        cotangent = jnp.concatenate([arrive[k] * error, arrive[k] * behind], axis=0)
        behind = jnp.sum(error * found_part[0:3], axis=0, keepdims=True) + found_part[3:4] * behind
        stack = jnp.concatenate(
            list(pieces(cotangent)) + [jnp.zeros((4, rays), F32)], axis=0
        ).astype(BF16)
        cot_b[0:16, k * rays : (k + 1) * rays] = stack
        cot_b[16:32, width + k * rays : width + (k + 1) * rays] = stack
    send3[:, 0:32] = dot_nt(onehot[...], cot_b[...])

    forth = direct(
        at, send3, last3, region_row, lambda y, x: at.opposite(y, x) * near + at.near,
        sends.at[3], receives.at[4],
    )
    forth.wait_recv()

    words = last3[...].T[0:32]
    given = [
        (words[q : q + 4] + words[q + 4 : q + 8]) + words[q + 8 : q + 12] for q in (0, 16)
    ]
    given = jnp.concatenate(
        [given[0][:, 0:lane], given[1][:, 0:lane], given[0][:, lane:], given[1][:, lane:]], axis=1
    )
    gain = given[0:1] * tone[0] + given[1:2] * tone[1] + given[2:3] * tone[2]
    after = given[3:4]
    backs = []
    for i in range(samples - 1, -1, -1):
        backs.append(befores[i] * (gain[i : i + 1] - after))
        after = alpha[i : i + 1] * gain[i : i + 1] + keep[i : i + 1] * after
    d_raw = [jnp.concatenate(backs[::-1], axis=0) * d_density]
    d_raw += [given[c : c + 1] * d_tone[c] for c in range(3)]
    for item in range(samples):
        half, first = divmod(2 * item, samples)
        for side in range(2):
            for k in range(4):
                graw_s[item, k : k + 1, side * part : (side + 1) * part] = d_raw[k][
                    first + side : first + side + 1, half * part : (half + 1) * part
                ]

    stores = [
        pltpu.make_async_copy(place, result, local.at[10 + index])
        for index, (place, result) in enumerate(zip(made, results))
    ]
    stores[0].start()
    backs = (wo, w3, w2)
    inputs = (lambda j: hidden[1, j], lambda j: hidden[0, j], lambda j: encoded[j])
    totals = (acc3, acc2, acc1)

    def gather(total, j, term):
        if j == 0:
            total[...] = term
        else:
            total[...] += term

    ends = (
        (3, g_head, lambda: acc4[0:4, :]),
        (2, g_hid.at[0, 1], lambda: acc3[...]),
        (2, g_hid.at[0, 0], lambda: acc2[...]),
        (1, g_in.at[0], lambda: acc1[...]),
    )
    for stage, j in staged(4, samples):
        if stage == 0:
            gather(acc4, j, dot_nt(graw_s[j].astype(BF16), hidden[2, j]))
        if stage < 3:
            g = graw_s[j].astype(BF16) if stage == 0 else cotangents[stage - 1, j]
            g = dot(backs[stage][...], g) * slope[2 - stage, j].astype(F32)
            cotangents[stage, j] = g.astype(BF16)
        if stage > 0:
            gather(totals[stage - 1], j, dot_nt(inputs[stage - 1](j), cotangents[stage - 1, j]))
        if j == samples - 1:
            index, place, value = ends[stage]
            place[...] = value().astype(BF16)
            if stage != 1:
                stores[index].start()

    for sent in (near1, *halves, back, forth):
        sent.wait_send()
    for store in stores:
        store.wait()


def hand_over(*refs):
    sources, results, places, sems = refs[:4], refs[4:8], refs[8:12], refs[12]
    width = sources[1].shape[1]
    half = width // 2
    pieces_of = [(0, ()), (3, ())]
    pieces_of += [(2, (0, k, pl.ds(h, half))) for k in range(2) for h in (0, half)]
    pieces_of += [(1, (0, pl.ds(h, half))) for h in (0, half)]

    def part(group, index, where):
        return group[index].at[where] if where else group[index]

    moves = [
        tuple(
            pltpu.make_async_copy(part(a, index, where), part(b, index, where), sems.at[row, number])
            for row, (a, b) in enumerate(((sources, places), (places, results)))
        )
        for number, (index, where) in enumerate(pieces_of)
    ]
    for load, _ in moves:
        load.start()
    for load, store in moves:
        load.wait()
        store.start()
    for _, store in moves:
        store.wait()


def per_device(
    anchors, directions, targets, region_ids, sample_counts, depth_index, frequencies,
    w_input, w_hidden, w_head,
):
    groups, regs = lax.axis_size("grp"), lax.axis_size("reg")
    rays, segs = region_ids.shape
    samples = depth_index.shape[2]
    width = w_input.shape[1]
    zn = min(CHIPS_Z, regs)
    n = groups * regs
    slots = 2 * n
    near, far = groups * zn, regs // zn
    lanes = segs * rays
    board = [pltpu.VMEM((n, LANES), BF16)] * 4 + [pltpu.VMEM((n, LANES), F32)] * 5
    square = (width, width)
    operands = (
        anchors, directions, targets, region_ids.T, sample_counts.T,
        depth_index.transpose(1, 2, 0), frequencies, w_input, w_hidden, w_head[0].T,
    )
    shapes = (
        jax.ShapeDtypeStruct((3, rays), F32),
        jax.ShapeDtypeStruct(w_input.shape, BF16),
        jax.ShapeDtypeStruct(w_hidden.shape, BF16),
        jax.ShapeDtypeStruct((4, width), BF16),
    )
    scratch = [pltpu.VMEM(x.shape, x.dtype) for x in operands] + board + [
        pltpu.VMEM((8, lanes), jnp.int32),
        pltpu.VMEM((32, lanes), F32),
        pltpu.VMEM((LANES, 2 * lanes), BF16),
        pltpu.VMEM((n, 2 * lanes), BF16),
        pltpu.VMEM((8, width // 2), F32),
        pltpu.VMEM((32, slots), F32),
        pltpu.VMEM((width // 2, slots), F32),
        pltpu.VMEM((width // 2, slots), F32),
        pltpu.VMEM((samples, slots), F32),
        pltpu.VMEM((16, width), F32),
        pltpu.VMEM((4, samples, slots), F32),
        pltpu.VMEM((samples, 16, slots), F32),
        pltpu.VMEM((32, 2 * lanes), BF16),
        pltpu.VMEM(square, BF16),
        pltpu.VMEM(square, BF16),
        pltpu.VMEM(square, BF16),
        pltpu.VMEM(square, BF16),
        pltpu.VMEM(square, BF16),
        pltpu.VMEM((16, width), BF16),
        pltpu.VMEM((width, 16), BF16),
        pltpu.VMEM((samples, width, slots), BF16),
        pltpu.VMEM((3, samples, width, slots), BF16),
        pltpu.VMEM((3, samples, width, slots), BF16),
        pltpu.VMEM((3, samples, width, slots), BF16),
        pltpu.VMEM(square, F32),
        pltpu.VMEM(square, F32),
        pltpu.VMEM(square, F32),
        pltpu.VMEM((16, width), F32),
    ] + [pltpu.VMEM(x.shape, x.dtype) for x in shapes] + [
        pltpu.SemaphoreType.DMA((4,)),
        pltpu.SemaphoreType.DMA((5,)),
        pltpu.SemaphoreType.DMA((14,)),
    ]
    whole = pl.BlockSpec(memory_space=pltpu.HBM)
    made = pl.pallas_call(
        functools.partial(kernel, (groups, regs, zn, rays, segs, samples)),
        out_shape=shapes,
        in_specs=[whole] * 10,
        out_specs=[whole] * 4,
        scratch_shapes=scratch,
        compiler_params=pltpu.CompilerParams(
            collective_id=0, has_side_effects=True, vmem_limit_bytes=VMEM_BYTES
        ),
        name="radiance_step",
    )(*operands)
    colours, g_in, g_hid, g_head = pl.pallas_call(
        hand_over,
        out_shape=shapes,
        in_specs=[whole] * 4,
        out_specs=[whole] * 4,
        scratch_shapes=[pltpu.VMEM(x.shape, x.dtype) for x in shapes]
        + [pltpu.SemaphoreType.DMA((2, 8))],
        name="hand_over",
    )(*made)
    return colours, g_in, g_hid, g_head.T[None]


def solution(mesh):
    both = ("grp", "reg")
    return jax.shard_map(
        per_device,
        mesh=mesh,
        in_specs=(
            P(None, both), P(None, both), P(None, both), P(both, None), P(both, None),
            P(both, None, None), P(), P(both, None, None), P(both, None, None, None),
            P(both, None, None),
        ),
        out_specs=(
            P(None, both), P(both, None, None), P(both, None, None, None), P(both, None, None),
        ),
        check_vma=False,
    )
```
